256 devices in a mesh: expert: 64 (over z, y, core), dp: 4 (over x).
Axes of the slice: x: 4, y: 4, z: 8, core: 2. Of those that a mesh axis runs over, the one named last changes fastest.
Arguments:
- tokens: bfloat16 [8192, 4096], P('expert', 'dp'), may hold values from -6 to 6
- to_latent: bfloat16 [4096, 1024], P('dp'), may hold values from -0.09375 to 0.09375
- from_latent: bfloat16 [1024, 4096], P(None, 'dp'), may hold values from -0.1875 to 0.1875
- expert_gate: bfloat16 [64, 1024, 2048], P('expert', None, 'dp'), may hold values from -0.1875 to 0.1875
- expert_up: bfloat16 [64, 1024, 2048], P('expert', None, 'dp'), may hold values from -0.1875 to 0.1875
- expert_down: bfloat16 [64, 2048, 1024], P('expert', 'dp'), may hold values from -0.125 to 0.125
- routes: int32 [8192, 8], P('expert'), may hold values from 0 to 63, as said below
- slot_index: int32 [8192, 8], P('expert'), may hold values from 0 to 20, as said below
- route_gates: float32 [8192, 8], P('expert'), may hold values from 0.05 to 0.5
- grad_output: bfloat16 [8192, 4096], P('expert', 'dp'), may hold values from -6 to 6
Outputs:
- layer_output: bfloat16 [8192, 4096], P('expert', 'dp')
- grad_tokens: bfloat16 [8192, 4096], P('expert', 'dp')
- grad_to_latent: float32 [1024, 4096], P('expert', 'dp')
- grad_from_latent: float32 [1024, 4096], P('expert', 'dp')
- grad_gate: bfloat16 [64, 1024, 2048], P('expert', None, 'dp')
- grad_up: bfloat16 [64, 1024, 2048], P('expert', None, 'dp')
- grad_down: bfloat16 [64, 2048, 1024], P('expert', 'dp')
The draws below stay inside these ranges and needn't reach their ends.
Inputs may be any that keep to these rules, and one draw needn't show every extreme that they name: `routes`: each row names 8 different experts. `slot_index`: among the routes of one device (aligned blocks of 128 rows) that name the same expert, slots count 0, 1, 2, ... in an order of that device's routes drawn from the seed; routes past the capacity hold 20 and are dropped. On every device some expert is named by more than 20 rows.
All inputs are finite; a program needn't handle non-finite values.
Results may differ from the reference program's by a relative error of at most 0.03.
Values may be sent and summed in bfloat16 or wider, within the bound.
A program may use at most 128 MiB of HBM per device.

```python
import jax
import jax.numpy as jnp
from jax import lax

D = 4096
L = 1024
H = 2048
TOP = 8
TOK_DEV = 128
EXPERTS = 64
TOKENS = 8192
CAP = 20
N_EXPERT = 64
N_DP = 4


def route_table(key):
    key_score, key_bias, key_hot, key_pick, key_order = jax.random.split(key, 5)
    expert_ids = jnp.arange(EXPERTS, dtype=jnp.int32)
    bias_level = jax.random.randint(key_bias, (EXPERTS,), 0, 600)
    hot_expert = jax.random.randint(key_hot, (), 0, EXPERTS)
    pick_keys = jax.random.randint(key_pick, (N_EXPERT, TOK_DEV), 0, 1048576) * TOK_DEV + jnp.arange(TOK_DEV, dtype=jnp.int32)[None, :]
    pick_rank = jnp.argsort(jnp.argsort(pick_keys, axis=1, stable=True), axis=1, stable=True).reshape(TOKENS)
    chosen_hot = (pick_rank < TOK_DEV // 2)[:, None] & (expert_ids[None, :] == hot_expert)
    scores = jax.random.randint(key_score, (TOKENS, EXPERTS), 0, 1000) + bias_level[None, :]
    scores = (scores + jnp.where(chosen_hot, 4000, 0)) * EXPERTS + expert_ids[None, :]
    top_scores, chosen = lax.top_k(scores, TOP)
    chosen = chosen.astype(jnp.int32)
    onehot = (chosen[:, :, None] == expert_ids[None, None, :]).astype(jnp.int32)
    grouped = onehot.reshape(N_EXPERT, TOK_DEV * TOP, EXPERTS)
    route_total = TOK_DEV * TOP
    order_keys = jax.random.randint(key_order, (N_EXPERT, route_total), 0, 32768) * route_total + jnp.arange(route_total, dtype=jnp.int32)[None, :]
    ordering = jnp.argsort(order_keys, axis=1, stable=True).astype(jnp.int32)
    inverse = jnp.argsort(ordering, axis=1, stable=True).astype(jnp.int32)
    permuted = jnp.take_along_axis(grouped, ordering[:, :, None], axis=1)
    earlier = jnp.cumsum(permuted, axis=1) - permuted
    rank_permuted = jnp.sum(earlier * permuted, axis=2)
    ranking = jnp.take_along_axis(rank_permuted, inverse, axis=1).reshape(TOKENS, TOP)
    return (chosen, jnp.minimum(ranking, CAP).astype(jnp.int32))


def draw_routes(key, part):
    return route_table(key)[0]


def draw_slot_index(key, part):
    return route_table(key)[1]


def block_scale(own_key, shape, shards, least, largest):
    level = 1.0
    for dim, parts in shards:
        heights = jax.random.uniform(jax.random.fold_in(jax.random.fold_in(own_key, 6), dim), (parts,), jnp.float32, least / len(shards), largest / len(shards))
        level = level * jnp.repeat(jnp.exp(heights), shape[dim] // parts).reshape((-1,) + (1,) * (len(shape) - 1 - dim))
    return level


def bell_draw(own_key, dims, deviation, reach, cuts=(), kind=jnp.bfloat16):
    array = jax.random.normal(own_key, dims, jnp.float32) * deviation
    if len(cuts) > 0:
        array = block_scale(own_key, dims, cuts, -0.22, 0.18) * array
    return jnp.clip(array, min=-reach, max=reach).astype(kind)


def setup_inputs(seed: int = 0) -> dict:
    streams_of = jax.random.split(jax.random.key(seed), 11)
    tokens = bell_draw(streams_of[0], (TOKENS, D), 1.0, 6.0, ((0, 64), (1, 4)))
    to_latent = bell_draw(streams_of[1], (D, L), D ** -0.5, 0.09375, ((0, 4),))
    from_latent = bell_draw(streams_of[2], (L, D), L ** -0.5, 0.1875, ((1, 4),))
    expert_gate = bell_draw(streams_of[3], (EXPERTS, L, H), L ** -0.5, 0.1875, ((0, 64), (2, 4)))
    expert_up = bell_draw(streams_of[4], (EXPERTS, L, H), L ** -0.5, 0.1875, ((0, 64), (2, 4)))
    expert_down = bell_draw(streams_of[5], (EXPERTS, H, L), H ** -0.5, 0.125, ((0, 64), (1, 4)))
    routes = draw_routes(jax.random.fold_in(streams_of[10], 71), 0)
    slot_index = draw_slot_index(jax.random.fold_in(streams_of[10], 71), 0)
    route_gates = jnp.clip(0.05 + 0.45 * jax.random.uniform(streams_of[8], (TOKENS, TOP), jnp.float32) ** block_scale(streams_of[8], (TOKENS, TOP), ((0, 64),), -0.2, 0.2), 0.05, 0.5)
    grad_output = bell_draw(streams_of[9], (TOKENS, D), 1.0, 6.0, ((0, 64), (1, 4)))
    return dict(tokens=tokens, to_latent=to_latent, from_latent=from_latent, expert_gate=expert_gate, expert_up=expert_up, expert_down=expert_down, routes=routes, slot_index=slot_index, route_gates=route_gates, grad_output=grad_output)


def rounded(summand):
    return lax.optimization_barrier(summand.astype(jnp.bfloat16)).astype(jnp.float32)


def reference(tokens, to_latent, from_latent, expert_gate, expert_up, expert_down, routes, slot_index, route_gates, grad_output):
    scaling = TOKENS ** -0.5
    hidden_block = H // N_DP
    total_cells = EXPERTS * N_EXPERT * CAP
    kept_routes = slot_index < CAP
    source = (jnp.arange(TOKENS, dtype=jnp.int32) // TOK_DEV)[:, None]
    cell_index = jnp.where(kept_routes, (routes * N_EXPERT + source) * CAP + slot_index, total_cells).astype(jnp.int32)
    entries = jnp.full((total_cells + 1,), TOKENS * TOP, jnp.int32)
    entries = entries.at[cell_index.reshape(-1)].set(jnp.arange(TOKENS * TOP, dtype=jnp.int32))[:total_cells]

    latent = jnp.dot(tokens, to_latent, preferred_element_type=jnp.float32).astype(jnp.bfloat16)
    latent_pad = jnp.concatenate([latent, jnp.zeros((1, L), jnp.bfloat16)], axis=0)
    expert_rows = latent_pad[entries // TOP].reshape(EXPERTS, N_EXPERT * CAP, L)

    def forward_expert(operands):
        row_block, gate_mat, up_mat, down_mat = operands
        pre_gate = jnp.dot(row_block, gate_mat, preferred_element_type=jnp.float32)
        pre_up = jnp.dot(row_block, up_mat, preferred_element_type=jnp.float32)
        hidden = (pre_gate * jax.nn.sigmoid(pre_gate) * pre_up).astype(jnp.bfloat16)
        running = jnp.zeros((row_block.shape[0], L), jnp.float32)
        for block_index in range(N_DP):
            lower_edge = block_index * hidden_block
            running = running + rounded(jnp.dot(hidden[:, lower_edge:lower_edge + hidden_block], down_mat[lower_edge:lower_edge + hidden_block], preferred_element_type=jnp.float32))
        return running

    expert_out = lax.map(forward_expert, (expert_rows, expert_gate, expert_up, expert_down))
    out_rows = jnp.concatenate([expert_out.reshape(-1, L), jnp.zeros((1, L), jnp.float32)], axis=0)
    picked = out_rows[cell_index]
    mixed_latent = jnp.einsum("tk,tkl->tl", route_gates, picked).astype(jnp.bfloat16)
    layer_output = jnp.dot(mixed_latent, from_latent, preferred_element_type=jnp.float32).astype(jnp.bfloat16)

    mixed_grad = jnp.dot(grad_output, from_latent.T, preferred_element_type=jnp.float32).astype(jnp.bfloat16)
    grad_from_latent = jnp.dot(mixed_latent.T, grad_output, preferred_element_type=jnp.float32) * scaling
    route_grads = (route_gates[:, :, None] * mixed_grad.astype(jnp.float32)[:, None, :]).astype(jnp.bfloat16)
    grad_pad = jnp.concatenate([route_grads.reshape(-1, L), jnp.zeros((1, L), jnp.bfloat16)], axis=0)
    grad_rows = grad_pad[entries].reshape(EXPERTS, N_EXPERT * CAP, L)

    def backward_expert(operands):
        row_block, grad_block, gate_mat, up_mat, down_mat = operands
        pre_gate = jnp.dot(row_block, gate_mat, preferred_element_type=jnp.float32)
        pre_up = jnp.dot(row_block, up_mat, preferred_element_type=jnp.float32)
        sigmoid_gate = jax.nn.sigmoid(pre_gate)
        activated = pre_gate * sigmoid_gate
        hidden = (activated * pre_up).astype(jnp.bfloat16)
        grad_hidden = jnp.dot(grad_block, down_mat.T, preferred_element_type=jnp.float32)
        grad_pre_gate = (grad_hidden * pre_up * (sigmoid_gate * (1.0 + pre_gate * (1.0 - sigmoid_gate)))).astype(jnp.bfloat16)
        grad_pre_up = (grad_hidden * activated).astype(jnp.bfloat16)
        running = jnp.zeros((row_block.shape[0], L), jnp.float32)
        for block_index in range(N_DP):
            lower_edge = block_index * hidden_block
            upper_edge = lower_edge + hidden_block
            block_sum = jnp.dot(grad_pre_gate[:, lower_edge:upper_edge], gate_mat[:, lower_edge:upper_edge].T, preferred_element_type=jnp.float32)
            block_sum = block_sum + jnp.dot(grad_pre_up[:, lower_edge:upper_edge], up_mat[:, lower_edge:upper_edge].T, preferred_element_type=jnp.float32)
            running = running + rounded(block_sum)
        gate_grad = (jnp.dot(row_block.T, grad_pre_gate, preferred_element_type=jnp.float32) * scaling).astype(jnp.bfloat16)
        up_grad = (jnp.dot(row_block.T, grad_pre_up, preferred_element_type=jnp.float32) * scaling).astype(jnp.bfloat16)
        down_grad = (jnp.dot(hidden.T, grad_block, preferred_element_type=jnp.float32) * scaling).astype(jnp.bfloat16)
        return running, gate_grad, up_grad, down_grad

    grad_expert_rows, grad_gate, grad_up, grad_down = lax.map(backward_expert, (expert_rows, grad_rows, expert_gate, expert_up, expert_down))
    back_rows = jnp.concatenate([grad_expert_rows.reshape(-1, L), jnp.zeros((1, L), jnp.float32)], axis=0)
    grad_latent = jnp.sum(back_rows[cell_index], axis=1).astype(jnp.bfloat16)
    grad_tokens = jnp.dot(grad_latent, to_latent.T, preferred_element_type=jnp.float32).astype(jnp.bfloat16)
    grad_to_latent = jnp.dot(grad_latent.T, tokens, preferred_element_type=jnp.float32) * scaling
    return (layer_output, grad_tokens, grad_to_latent, grad_from_latent, grad_gate, grad_up, grad_down)
```

```python
import functools

import jax
import jax.numpy as jnp
from jax import lax
from jax.experimental import pallas as pl
from jax.experimental.pallas import tpu as pltpu
from jax.sharding import PartitionSpec as P

F32 = jnp.float32
BF16 = jnp.bfloat16
LAST = (((1,), (1,)), ((), ()))
FIRST = (((0,), (0,)), ((), ()))
MESH = pl.DeviceIdType.MESH


def remote(src, dst, send_sem, recv_sem, where):
    return pltpu.make_async_remote_copy(
        src_ref=src, dst_ref=dst, send_sem=send_sem, recv_sem=recv_sem, device_id=where, device_id_type=MESH
    )


def layer_kernel(
    cfg,
    routes_ref,
    slots_ref,
    gates_ref,
    tok_in,
    tl_in,
    fl_in,
    gate_in,
    up_in,
    down_in,
    go_in,
    lo_out,
    gt_out,
    gg_out,
    gu_out,
    gd_out,
    mixed_out,
    glat_out,
    tok_v,
    tl_v,
    fl_v,
    gate_v,
    up_v,
    down_v,
    go_v,
    lo_v,
    gt_v,
    gg_v,
    gu_v,
    gd_v,
    mixed_v,
    glat_v,
    xs_send_v,
    xs_recv_v,
    s_tab,
    g_tab,
    pp,
    pph,
    ppl,
    perm,
    outgoing,
    arrived,
    leaving,
    returned,
    full,
    part,
    relay,
    frm,
    pg_v,
    pu_v,
    hid_v,
    gpg_v,
    gpu_v,
    load_sem,
    store_sem,
    xs_ssem,
    xs_rsem,
    a2a_ssem,
    a2a_rsem,
    ag_ssem,
    ag_rsem,
    rs_ssem,
    rs_rsem,
    fin_ssem,
    fin_rsem,
):
    n, T, R, L, Q, W, G, NG, NC = (cfg[k] for k in ("n", "T", "R", "L", "Q", "W", "G", "NG", "NC"))
    scaling = cfg["scaling"]
    R2 = 2 * R
    RG = G * R
    RC = n * R // NC
    GC = NG // NC
    me = lax.axis_index("expert")
    x = lax.axis_index("dp")
    right = lax.rem(x + 1, 4)
    left = lax.rem(x + 3, 4)
    opp = lax.rem(x + 2, 4)
    peers = (right, left, opp)

    loads = [
        pltpu.make_async_copy(src, dst, load_sem.at[i])
        for i, (src, dst) in enumerate(
            (
                (tok_in, tok_v),
                (tl_in, tl_v),
                (go_in, go_v),
                (fl_in, fl_v),
                (gate_in.at[0], gate_v),
                (up_in.at[0], up_v),
                (down_in.at[0], down_v),
            )
        )
    ]
    for load in loads:
        load.start()
    barrier = pltpu.get_barrier_semaphore()
    for peer in peers:
        pl.semaphore_signal(barrier, inc=1, device_id={"dp": peer}, device_id_type=MESH)

    @pl.loop(1, n)
    def _(k):
        pl.semaphore_signal(barrier, inc=1, device_id={"expert": lax.rem(me + k, n)}, device_id_type=MESH)

    krel = lax.broadcasted_iota(jnp.int32, (n, T), 0)
    s_val = jnp.full((n, T), -1000, jnp.int32)
    g_val = jnp.zeros((n, T), F32)
    for j in range(routes_ref.shape[0]):
        rel = routes_ref[j : j + 1, :] - me
        rel = jnp.where(rel < 0, rel + n, rel)
        slot = slots_ref[j : j + 1, :]
        match = (krel == rel) & (slot < R)
        s_val = jnp.where(match, slot, s_val)
        g_val = jnp.where(match, gates_ref[j : j + 1, :], g_val)
    s_tab[...] = s_val
    g_tab[...] = g_val

    size = 4 * R2
    row = lax.broadcasted_iota(jnp.int32, (size, size), 0)
    col = lax.broadcasted_iota(jnp.int32, (size, size), 1)
    kk = jnp.where(row >= 2 * R2, jnp.where(row >= 3 * R2, 3, 2), jnp.where(row >= R2, 1, 0))
    rest = row - kk * R2
    half = jnp.where(rest >= R, 1, 0)
    perm[0] = jnp.where(col == half * (4 * R) + kk * R + rest - half * R, 1.0, 0.0).astype(BF16)
    kk = jnp.where(col >= 2 * R2, jnp.where(col >= 3 * R2, 3, 2), jnp.where(col >= R2, 1, 0))
    rest = col - kk * R2
    half = jnp.where(rest >= R, 1, 0)
    perm[1] = jnp.where(row == half * (4 * R) + kk * R + rest - half * R, 1.0, 0.0).astype(BF16)

    def xs_copy(ph, j):
        return remote(
            xs_send_v.at[ph, j], xs_recv_v.at[ph, x], xs_ssem.at[ph, j], xs_rsem.at[ph, x], {"dp": j}
        )

    def xs_start(ph, value):
        for j in range(4):
            xs_send_v[ph, j] = value[:, j * Q : (j + 1) * Q].astype(BF16)
        for peer in peers:
            xs_copy(ph, peer).start()

    def xs_finish(ph):
        total = xs_send_v[ph, x].astype(F32)
        for peer in peers:
            remote(
                xs_send_v.at[ph, x], xs_recv_v.at[ph, peer], xs_ssem.at[ph, peer], xs_rsem.at[ph, peer], {"dp": peer}
            ).wait_recv()
            total = total + xs_recv_v[ph, peer].astype(F32)
        total = total.astype(BF16)
        return jnp.concatenate([total[:, :W], total[:, W:]], axis=0)

    loads[0].wait()
    loads[1].wait()
    latent_part = jnp.dot(tok_v[...], tl_v[...], preferred_element_type=F32)
    pl.semaphore_wait(barrier, n - 1 + 3)
    xs_start(0, latent_part)
    loads[2].wait()
    loads[3].wait()
    xs_start(1, lax.dot_general(go_v[...], fl_v[...], LAST, preferred_element_type=F32))

    r_iota = lax.broadcasted_iota(jnp.int32, (G, R2, T), 1)

    @pl.loop(0, NG)
    def _(g):
        ks = pl.ds(pl.multiple_of(g * G, G), G)
        rows = pl.ds(pl.multiple_of(g * G * R2, G * R2), G * R2)
        s8 = jnp.broadcast_to(s_tab[ks, :].reshape(G, 1, T), (G, R2, T))
        g8 = jnp.broadcast_to(g_tab[ks, :].reshape(G, 1, T), (G, R2, T))
        g_hi = g8.astype(BF16).astype(F32)
        g_lo = g8 - g_hi
        for h in range(2):
            match = s8 == r_iota - h * R
            lanes = slice(h * T, (h + 1) * T)
            pp[rows, lanes] = jnp.where(match, 1.0, 0.0).reshape(G * R2, T).astype(BF16)
            pph[rows, lanes] = jnp.where(match, g_hi, 0.0).reshape(G * R2, T).astype(BF16)
            ppl[rows, lanes] = jnp.where(match, g_lo, 0.0).reshape(G * R2, T).astype(BF16)

    def dispatch(ph, stacked):
        @pl.loop(0, NG)
        def _(g):
            ks = pl.ds(pl.multiple_of(g * G, G), G)
            rows = pl.ds(pl.multiple_of(g * G * R2, G * R2), G * R2)
            if ph == 0:
                block = jnp.dot(pp[rows, :], stacked, preferred_element_type=F32)
            else:
                block = jnp.dot(pph[rows, :], stacked, preferred_element_type=F32)
                block = block + jnp.dot(ppl[rows, :], stacked, preferred_element_type=F32)
            outgoing[ph, ks] = block.reshape(G, R2, W).astype(BF16)

            @pl.loop(jnp.maximum(g * G, 1), g * G + G)
            def _(k):
                remote(
                    outgoing.at[ph, k],
                    arrived.at[ph, k],
                    a2a_ssem.at[ph],
                    a2a_rsem.at[ph, g],
                    {"expert": lax.rem(me + k, n)},
                ).start()

        arrived[ph, 0] = outgoing[ph, 0]

    dispatch(0, xs_finish(0))
    dispatch(1, xs_finish(1))

    def a2a_wait(ph, buf, g):
        @pl.when(g == 0)
        def _():
            pltpu.make_async_copy(buf.at[1:G], buf.at[1:G], a2a_rsem.at[ph, 0]).wait()

        @pl.when(g != 0)
        def _():
            ks = pl.ds(pl.multiple_of(g * G, G), G)
            pltpu.make_async_copy(buf.at[ks], buf.at[ks], a2a_rsem.at[ph, g]).wait()

    def group_rows(g):
        return pl.ds(pl.multiple_of(g * RG, RG), RG)

    halves = (slice(0, W), slice(W, 2 * W))

    def ag_copy(ph, g, kind, q):
        src = full.at[ph, q, group_rows(g)]
        if kind >= 2:
            src = full.at[ph, q, group_rows(g), halves[kind - 2]]
        where = {"dp": right if kind % 2 == 0 else left}
        return remote(src, src, ag_ssem.at[ph, g, kind], ag_rsem.at[ph, g, kind], where)

    def ag_start(ph, g):
        a2a_wait(ph, arrived.at[ph], g)
        for sub in range(G // 4):
            ks = pl.ds(pl.multiple_of(g * G + sub * 4, 4), 4)
            block = arrived[ph, ks].astype(F32).reshape(4 * R2, W).astype(BF16)
            dense = jnp.dot(perm[1], block, preferred_element_type=F32).astype(BF16)
            rows = pl.ds(pl.multiple_of(g * RG + sub * 4 * R, 4 * R), 4 * R)
            full[ph, x, rows, 0:W] = dense[: 4 * R]
            full[ph, x, rows, W : 2 * W] = dense[4 * R :]
        ag_copy(ph, g, 0, x).start()
        ag_copy(ph, g, 1, x).start()

    def ag_forward(ph, g):
        ag_copy(ph, g, 0, left).wait_recv()
        ag_copy(ph, g, 2, left).start()
        ag_copy(ph, g, 1, right).wait_recv()
        ag_copy(ph, g, 3, right).start()

    def ag_finish(ph, g):
        ag_copy(ph, g, 2, opp).wait_recv()
        ag_copy(ph, g, 3, opp).wait_recv()

    def chunk_rows(c):
        return pl.ds(pl.multiple_of(c * RC, RC), RC)

    def rs_copy(ph, c, kind):
        rows = chunk_rows(c)
        src, dst, where = (
            (part.at[ph, opp, rows, halves[0]], relay.at[ph, 0, rows], left),
            (part.at[ph, opp, rows, halves[1]], relay.at[ph, 1, rows], right),
            (part.at[ph, left, rows, halves[1]], frm.at[ph, 1, rows, halves[1]], left),
            (part.at[ph, right, rows, halves[0]], frm.at[ph, 0, rows, halves[0]], right),
            (part.at[ph, left, rows, halves[0]], frm.at[ph, 1, rows, halves[0]], left),
            (part.at[ph, right, rows, halves[1]], frm.at[ph, 0, rows, halves[1]], right),
        )[kind]
        return remote(src, dst, rs_ssem.at[ph, c, kind], rs_rsem.at[ph, c, kind], {"dp": where})

    def rs_start(ph, c, value):
        for j in range(4):
            part[ph, j, chunk_rows(c)] = value[:, j * Q : (j + 1) * Q].astype(BF16)
        for kind in range(4):
            rs_copy(ph, c, kind).start()

    def rs_relay(ph, c):
        rows = chunk_rows(c)
        for kind, target in ((0, left), (1, right)):
            rs_copy(ph, c, kind).wait_recv()
            own = part[ph, target, rows, halves[kind]].astype(F32)
            part[ph, target, rows, halves[kind]] = (own + relay[ph, kind, rows].astype(F32)).astype(BF16)
            rs_copy(ph, c, 4 + kind).start()

    def rs_finish(ph, c):
        for kind in (2, 3, 4, 5):
            rs_copy(ph, c, kind).wait_recv()

        @pl.loop(0, GC * G // 4)
        def _(sub):
            base = c * (GC * G) + sub * 4
            rows = pl.ds(pl.multiple_of(base * R, 4 * R), 4 * R)
            total = part[ph, x, rows].astype(F32) + frm[ph, 0, rows].astype(F32) + frm[ph, 1, rows].astype(F32)
            total = total.astype(BF16)
            stacked = jnp.concatenate([total[:, :W], total[:, W:]], axis=0)
            block = jnp.dot(perm[0], stacked, preferred_element_type=F32)
            leaving[ph, pl.ds(pl.multiple_of(base, 4), 4)] = block.reshape(4, R2, W).astype(BF16)

            @pl.loop(jnp.maximum(base, 1), base + 4)
            def _(k):
                remote(
                    leaving.at[ph, k],
                    returned.at[ph, k],
                    a2a_ssem.at[2 + ph],
                    a2a_rsem.at[2 + ph, lax.div(k, G)],
                    {"expert": lax.rem(me + n - k, n)},
                ).start()

    def fwd(c):
        rows = chunk_rows(c)
        block = jnp.concatenate([full[0, j, rows] for j in range(4)], axis=1)
        pre_gate = jnp.dot(block, gate_v[...], preferred_element_type=F32)
        pre_up = jnp.dot(block, up_v[...], preferred_element_type=F32)
        pg_v[rows, :] = pre_gate
        pu_v[rows, :] = pre_up
        hidden = (pre_gate * jax.nn.sigmoid(pre_gate) * pre_up).astype(BF16)
        hid_v[rows, :] = hidden
        return jnp.dot(hidden, down_v[...], preferred_element_type=F32)

    def bwd(c):
        rows = chunk_rows(c)
        block = jnp.concatenate([full[1, j, rows] for j in range(4)], axis=1)
        grad_hidden = lax.dot_general(block, down_v[...], LAST, preferred_element_type=F32)
        pre_gate = pg_v[rows, :]
        pre_up = pu_v[rows, :]
        s = jax.nn.sigmoid(pre_gate)
        grad_gate = (grad_hidden * pre_up * (s * (1.0 + pre_gate * (1.0 - s)))).astype(BF16)
        grad_up = (grad_hidden * (pre_gate * s)).astype(BF16)
        gpg_v[rows, :] = grad_gate
        gpu_v[rows, :] = grad_up
        value = lax.dot_general(grad_gate, gate_v[...], LAST, preferred_element_type=F32)
        return value + lax.dot_general(grad_up, up_v[...], LAST, preferred_element_type=F32)

    @pl.loop(0, NG)
    def _(g):
        ag_start(0, g)

        @pl.when(g > 0)
        def _():
            ag_forward(0, g - 1)

    ag_forward(0, NG - 1)
    for load in loads[4:]:
        load.wait()

    @pl.loop(0, NC)
    def _(c):
        for i in range(GC):
            g = c * GC + i
            ag_start(1, g)

            @pl.when(g > 0)
            def _():
                ag_forward(1, g - 1)

        for i in range(GC):
            ag_finish(0, c * GC + i)
        rs_start(0, c, fwd(c))

        @pl.when(c > 0)
        def _():
            rs_relay(0, c - 1)

    ag_forward(1, NG - 1)
    rs_relay(0, NC - 1)

    @pl.loop(0, NC)
    def _(c):
        for i in range(GC):
            ag_finish(1, c * GC + i)
        rs_start(1, c, bwd(c))
        rs_finish(0, c)

        @pl.when(c > 0)
        def _():
            rs_relay(1, c - 1)

    rs_relay(1, NC - 1)
    returned[0, 0] = leaving[0, 0]

    @pl.loop(0, NC)
    def _(c):
        rs_finish(1, c)

    returned[1, 0] = leaving[1, 0]

    def combine(ph, weights):
        total = jnp.zeros((2 * T, W), F32)

        def step(g, total):
            a2a_wait(2 + ph, returned.at[ph], g)
            ks = pl.ds(pl.multiple_of(g * G, G), G)
            rows = pl.ds(pl.multiple_of(g * G * R2, G * R2), G * R2)
            block = returned[ph, ks].astype(F32).reshape(G * R2, W).astype(BF16)
            for weight in weights:
                total = total + lax.dot_general(weight[rows, :], block, FIRST, preferred_element_type=F32)
            return total

        total = lax.fori_loop(0, NG, step, total)
        return jnp.concatenate([total[:T], total[T:]], axis=1).astype(BF16)

    def lanes_of(q):
        return pl.ds(pl.multiple_of(q * Q, Q), Q)

    def fin_copy(ph, ref, q, peer, slot):
        src = ref.at[:, lanes_of(q)]
        return remote(src, src, fin_ssem.at[ph, peer], fin_rsem.at[ph, slot], {"dp": peer})

    def fin_start(ph, ref, value):
        ref[:, lanes_of(x)] = value
        for peer in peers:
            fin_copy(ph, ref, x, peer, x).start()

    def fin_finish(ph, ref):
        for peer in peers:
            fin_copy(ph, ref, peer, peer, peer).wait_recv()

    stores = []

    def store(src, dst):
        copy = pltpu.make_async_copy(src, dst, store_sem.at[len(stores)])
        copy.start()
        stores.append(copy)

    fin_start(0, mixed_v, combine(0, (pph, ppl)))

    @pl.loop(0, 4)
    def _(j):
        rows = pl.ds(pl.multiple_of(j * Q, Q), Q)
        block = full[0, j]
        gg_v[rows, :] = (lax.dot_general(block, gpg_v[...], FIRST, preferred_element_type=F32) * scaling).astype(BF16)
        gu_v[rows, :] = (lax.dot_general(block, gpu_v[...], FIRST, preferred_element_type=F32) * scaling).astype(BF16)
        gd_v[:, rows] = (
            lax.dot_general(hid_v[...], full[1, j], FIRST, preferred_element_type=F32) * scaling
        ).astype(BF16)

    store(gg_v, gg_out.at[0])
    store(gu_v, gu_out.at[0])
    store(gd_v, gd_out.at[0])
    fin_start(1, glat_v, combine(1, (pp,)))
    fin_finish(0, mixed_v)
    store(mixed_v, mixed_out)
    lo_v[...] = jnp.dot(mixed_v[...], fl_v[...], preferred_element_type=F32).astype(BF16)
    store(lo_v, lo_out)
    fin_finish(1, glat_v)
    store(glat_v, glat_out)
    gt_v[...] = lax.dot_general(glat_v[...], tl_v[...], LAST, preferred_element_type=F32).astype(BF16)
    store(gt_v, gt_out)

    for ph in range(2):
        for peer in peers:
            xs_copy(ph, peer).wait_send()
        fin_ref = (mixed_v, glat_v)[ph]
        for peer in peers:
            fin_copy(ph, fin_ref, x, peer, x).wait_send()
        for buf, sem in ((outgoing.at[ph], a2a_ssem.at[ph]), (leaving.at[ph], a2a_ssem.at[2 + ph])):
            pltpu.make_async_copy(buf.at[1:n], buf.at[1:n], sem).wait()

        @pl.loop(0, NG)
        def _(g):
            for kind, q in ((0, x), (1, x), (2, left), (3, right)):
                ag_copy(ph, g, kind, q).wait_send()

        @pl.loop(0, NC)
        def _(c):
            for kind in range(6):
                rs_copy(ph, c, kind).wait_send()

    for copy in stores:
        copy.wait()


def layer_call(capacity, n, routes, slot_index, route_gates, tokens, to_latent, from_latent, gate, up, down, grad_output):
    T, Dd = tokens.shape
    L = to_latent.shape[1]
    Hs = gate.shape[2]
    Q, W = L // 4, L // 8
    R = capacity
    G = 8 if n >= 16 else 4
    NG = n // G
    NC = min(4, NG)
    cfg = dict(n=n, T=T, R=R, L=L, Q=Q, W=W, G=G, NG=NG, NC=NC, scaling=float((T * n) ** -0.5))
    rows = n * R
    vm = lambda shape, dtype=BF16: pltpu.VMEM(shape, dtype)
    dma = lambda *shape: pltpu.SemaphoreType.DMA(shape)
    any_spec = pl.BlockSpec(memory_space=pl.ANY)
    vm_spec = pl.BlockSpec(memory_space=pltpu.VMEM)
    outs = [
        ((T, Dd), BF16),
        ((T, Dd), BF16),
        (gate.shape, BF16),
        (up.shape, BF16),
        (down.shape, BF16),
        ((T, L), BF16),
        ((T, L), BF16),
    ]
    scratch = [
        vm((T, Dd)),
        vm((Dd, L)),
        vm((L, Dd)),
        vm((L, Hs)),
        vm((L, Hs)),
        vm((Hs, L)),
        vm((T, Dd)),
        vm((T, Dd)),
        vm((T, Dd)),
        vm((L, Hs)),
        vm((L, Hs)),
        vm((Hs, L)),
        vm((T, L)),
        vm((T, L)),
        vm((2, 4, T, Q)),
        vm((2, 4, T, Q)),
        vm((n, T), jnp.int32),
        vm((n, T), F32),
        vm((2 * rows, 2 * T)),
        vm((2 * rows, 2 * T)),
        vm((2 * rows, 2 * T)),
        vm((2, 8 * R, 8 * R)),
        vm((2, n, 2 * R, W)),
        vm((2, n, 2 * R, W)),
        vm((2, n, 2 * R, W)),
        vm((2, n, 2 * R, W)),
        vm((2, 4, rows, Q)),
        vm((2, 4, rows, Q)),
        vm((2, 2, rows, W)),
        vm((2, 2, rows, Q)),
        vm((rows, Hs), F32),
        vm((rows, Hs), F32),
        vm((rows, Hs)),
        vm((rows, Hs)),
        vm((rows, Hs)),
        dma(7),
        dma(7),
        dma(2, 4),
        dma(2, 4),
        dma(4),
        dma(4, NG),
        dma(2, NG, 4),
        dma(2, NG, 4),
        dma(2, NC, 6),
        dma(2, NC, 6),
        dma(2, 4),
        dma(2, 4),
    ]
    flops = 2 * rows * L * Hs * 9 + 2 * T * L * Dd * 4
    return pl.pallas_call(
        functools.partial(layer_kernel, cfg),
        out_shape=[jax.ShapeDtypeStruct(s, d) for s, d in outs],
        in_specs=[vm_spec] * 3 + [any_spec] * 7,
        out_specs=[any_spec] * len(outs),
        scratch_shapes=scratch,
        compiler_params=pltpu.CompilerParams(
            collective_id=0, has_side_effects=True, vmem_limit_bytes=62 * 1024 * 1024
        ),
        cost_estimate=pl.CostEstimate(flops=flops, bytes_accessed=16 * 2**20, transcendentals=rows * Hs),
    )(routes.T, slot_index.T, route_gates.T, tokens, to_latent, from_latent, gate, up, down, grad_output)


def spread_grad(left_side, right_side, scaling):
    return lax.psum_scatter(
        lax.dot_general(left_side, right_side, FIRST, preferred_element_type=F32) * scaling,
        "expert",
        scatter_dimension=0,
        tiled=True,
    )


def local(
    tokens,
    to_latent,
    from_latent,
    expert_gate,
    expert_up,
    expert_down,
    routes,
    slot_index,
    route_gates,
    grad_output,
):
    expert_count = lax.axis_size("expert")
    dp_count = lax.axis_size("dp")
    token_count, route_count = routes.shape
    capacity = dp_count * max(
        1,
        min(
            token_count // (4 * dp_count),
            5 * token_count * route_count // (4 * expert_count * dp_count),
        ),
    )
    scaling = (token_count * expert_count) ** (-0.5)
    layer_output, grad_tokens, grad_gate, grad_up, grad_down, mixed, grad_latent = layer_call(
        capacity,
        expert_count,
        routes,
        slot_index,
        route_gates,
        tokens,
        to_latent,
        from_latent,
        expert_gate,
        expert_up,
        expert_down,
        grad_output,
    )
    grad_from_latent = spread_grad(mixed, grad_output, scaling)
    grad_to_latent = spread_grad(grad_latent, tokens, scaling)
    return (
        layer_output,
        grad_tokens,
        grad_to_latent,
        grad_from_latent,
        grad_gate,
        grad_up,
        grad_down,
    )


def solution(mesh):
    return jax.shard_map(
        local,
        mesh=mesh,
        in_specs=(
            P("expert", "dp"),
            P("dp", None),
            P(None, "dp"),
            P("expert", None, "dp"),
            P("expert", None, "dp"),
            P("expert", "dp", None),
            P("expert", None),
            P("expert", None),
            P("expert", None),
            P("expert", "dp"),
        ),
        out_specs=(
            P("expert", "dp"),
            P("expert", "dp"),
            P("expert", "dp"),
            P("expert", "dp"),
            P("expert", None, "dp"),
            P("expert", None, "dp"),
            P("expert", "dp", None),
        ),
        check_vma=False,
    )
```

```python
import functools

import jax
import jax.numpy as jnp
from jax import lax
from jax.experimental import pallas as pl
from jax.experimental.pallas import tpu as pltpu
from jax.sharding import PartitionSpec as P

F32 = jnp.float32
BF16 = jnp.bfloat16
LAST = (((1,), (1,)), ((), ()))
FIRST = (((0,), (0,)), ((), ()))
MESH = pl.DeviceIdType.MESH


def remote(src, dst, send_sem, recv_sem, where):
    return pltpu.make_async_remote_copy(
        src_ref=src, dst_ref=dst, send_sem=send_sem, recv_sem=recv_sem, device_id=where, device_id_type=MESH
    )


def layer_kernel(
    cfg,
    routes_ref,
    slots_ref,
    gates_ref,
    tok_in,
    tl_in,
    fl_in,
    gate_in,
    up_in,
    down_in,
    go_in,
    lo_out,
    gt_out,
    gg_out,
    gu_out,
    gd_out,
    gtl_out,
    gfl_out,
    tok_v,
    tl_v,
    fl_v,
    gate_v,
    up_v,
    down_v,
    go_v,
    lo_v,
    gt_v,
    gg_v,
    gu_v,
    gd_v,
    lat_v,
    sel_v,
    gpart,
    grelay,
    gfrm,
    zsend,
    zrecv,
    gsum,
    xs_send_v,
    xs_recv_v,
    s_tab,
    g_tab,
    pp,
    pph,
    ppl,
    perm,
    outgoing,
    arrived,
    leaving,
    returned,
    full,
    part,
    relay,
    frm,
    pg_v,
    pu_v,
    hid_v,
    gpg_v,
    gpu_v,
    load_sem,
    store_sem,
    xs_ssem,
    xs_rsem,
    a2a_ssem,
    a2a_rsem,
    ag_ssem,
    ag_rsem,
    rs_ssem,
    rs_rsem,
    fin_ssem,
    fin_rsem,
    sib_ssem,
    sib_rsem,
    ring_ssem,
    ring_rsem,
    z_ssem,
    z_rsem,
):
    Z, RB, Dd = cfg["Z"], cfg["RB"], cfg["Dd"]
    n, T, R, L, Q, W, G, NG, NC = (cfg[k] for k in ("n", "T", "R", "L", "Q", "W", "G", "NG", "NC"))
    scaling = cfg["scaling"]
    R2 = 2 * R
    RG = G * R
    RC = n * R // NC
    GC = NG // NC
    me = lax.axis_index("expert")
    x = lax.axis_index("dp")
    right = lax.rem(x + 1, 4)
    left = lax.rem(x + 3, 4)
    opp = lax.rem(x + 2, 4)
    peers = (right, left, opp)
    core = lax.rem(me, 2)
    y = lax.rem(lax.div(me, 2), 4)
    z = lax.div(me, 8)
    sibling = {"expert": me + 1 - 2 * core}

    def at_y(other):
        return {"expert": (z * 4 + other) * 2 + core}

    y_right = lax.rem(y + 1, 4)
    y_left = lax.rem(y + 3, 4)
    y_opp = lax.rem(y + 2, 4)

    loads = [
        pltpu.make_async_copy(src, dst, load_sem.at[i])
        for i, (src, dst) in enumerate(
            (
                (tok_in, tok_v.at[core]),
                (tl_in, tl_v),
                (go_in, go_v.at[core]),
                (fl_in, fl_v),
                (gate_in.at[0], gate_v),
                (up_in.at[0], up_v),
                (down_in.at[0], down_v),
            )
        )
    ]
    for load in loads:
        load.start()
    barrier = pltpu.get_barrier_semaphore()
    for peer in peers:
        pl.semaphore_signal(barrier, inc=1, device_id={"dp": peer}, device_id_type=MESH)

    @pl.loop(1, n)
    def _(k):
        pl.semaphore_signal(barrier, inc=1, device_id={"expert": lax.rem(me + k, n)}, device_id_type=MESH)

    krel = lax.broadcasted_iota(jnp.int32, (n, T), 0)
    s_val = jnp.full((n, T), -1000, jnp.int32)
    g_val = jnp.zeros((n, T), F32)
    for j in range(routes_ref.shape[0]):
        rel = routes_ref[j : j + 1, :] - me
        rel = jnp.where(rel < 0, rel + n, rel)
        slot = slots_ref[j : j + 1, :]
        match = (krel == rel) & (slot < R)
        s_val = jnp.where(match, slot, s_val)
        g_val = jnp.where(match, gates_ref[j : j + 1, :], g_val)
    s_tab[...] = s_val
    g_tab[...] = g_val

    size = 4 * R2
    row = lax.broadcasted_iota(jnp.int32, (size, size), 0)
    col = lax.broadcasted_iota(jnp.int32, (size, size), 1)
    kk = jnp.where(row >= 2 * R2, jnp.where(row >= 3 * R2, 3, 2), jnp.where(row >= R2, 1, 0))
    rest = row - kk * R2
    half = jnp.where(rest >= R, 1, 0)
    perm[0] = jnp.where(col == half * (4 * R) + kk * R + rest - half * R, 1.0, 0.0).astype(BF16)
    kk = jnp.where(col >= 2 * R2, jnp.where(col >= 3 * R2, 3, 2), jnp.where(col >= R2, 1, 0))
    rest = col - kk * R2
    half = jnp.where(rest >= R, 1, 0)
    perm[1] = jnp.where(row == half * (4 * R) + kk * R + rest - half * R, 1.0, 0.0).astype(BF16)

    def xs_copy(ph, j):
        return remote(
            xs_send_v.at[ph, j], xs_recv_v.at[ph, x], xs_ssem.at[ph, j], xs_rsem.at[ph, x], {"dp": j}
        )

    def xs_start(ph, value):
        for j in range(4):
            xs_send_v[ph, j] = value[:, j * Q : (j + 1) * Q].astype(BF16)
        for peer in peers:
            xs_copy(ph, peer).start()

    def xs_finish(ph):
        total = xs_send_v[ph, x].astype(F32)
        for peer in peers:
            remote(
                xs_send_v.at[ph, x], xs_recv_v.at[ph, peer], xs_ssem.at[ph, peer], xs_rsem.at[ph, peer], {"dp": peer}
            ).wait_recv()
            total = total + xs_recv_v[ph, peer].astype(F32)
        total = total.astype(BF16)
        return jnp.concatenate([total[:, :W], total[:, W:]], axis=0)

    def sib_copy(i):
        ref = (tok_v, go_v)[i].at[core]
        return remote(ref, ref, sib_ssem.at[i], sib_rsem.at[i], sibling)

    loads[0].wait()
    loads[1].wait()
    latent_part = jnp.dot(tok_v[core], tl_v[...], preferred_element_type=F32)
    pl.semaphore_wait(barrier, n - 1 + 3)
    xs_start(0, latent_part)
    loads[2].wait()
    loads[3].wait()
    xs_start(1, lax.dot_general(go_v[core], fl_v[...], LAST, preferred_element_type=F32))
    sib_copy(0).start()
    sib_copy(1).start()

    srow = lax.broadcasted_iota(jnp.int32, (1, L // 2), 1)
    sy = lax.shift_right_logical(srow, (Z * RB).bit_length() - 1)
    sz = lax.shift_right_logical(srow, RB.bit_length() - 1) & (Z - 1)
    want = ((sz * 4 + sy) * 2 + core) * RB + (srow & (RB - 1))
    scol = lax.broadcasted_iota(jnp.int32, (L, L // 2), 0)
    sel_v[...] = jnp.where(scol == want, 1.0, 0.0).astype(BF16)

    r_iota = lax.broadcasted_iota(jnp.int32, (G, R2, T), 1)

    @pl.loop(0, NG)
    def _(g):
        ks = pl.ds(pl.multiple_of(g * G, G), G)
        rows = pl.ds(pl.multiple_of(g * G * R2, G * R2), G * R2)
        s8 = jnp.broadcast_to(s_tab[ks, :].reshape(G, 1, T), (G, R2, T))
        g8 = jnp.broadcast_to(g_tab[ks, :].reshape(G, 1, T), (G, R2, T))
        g_hi = g8.astype(BF16).astype(F32)
        g_lo = g8 - g_hi
        for h in range(2):
            match = s8 == r_iota - h * R
            lanes = slice(h * T, (h + 1) * T)
            pp[rows, lanes] = jnp.where(match, 1.0, 0.0).reshape(G * R2, T).astype(BF16)
            pph[rows, lanes] = jnp.where(match, g_hi, 0.0).reshape(G * R2, T).astype(BF16)
            ppl[rows, lanes] = jnp.where(match, g_lo, 0.0).reshape(G * R2, T).astype(BF16)

    def dispatch(ph, stacked):
        @pl.loop(0, NG)
        def _(g):
            ks = pl.ds(pl.multiple_of(g * G, G), G)
            rows = pl.ds(pl.multiple_of(g * G * R2, G * R2), G * R2)
            if ph == 0:
                block = jnp.dot(pp[rows, :], stacked, preferred_element_type=F32)
            else:
                block = jnp.dot(pph[rows, :], stacked, preferred_element_type=F32)
                block = block + jnp.dot(ppl[rows, :], stacked, preferred_element_type=F32)
            outgoing[ph, ks] = block.reshape(G, R2, W).astype(BF16)

            @pl.loop(jnp.maximum(g * G, 1), g * G + G)
            def _(k):
                remote(
                    outgoing.at[ph, k],
                    arrived.at[ph, k],
                    a2a_ssem.at[ph],
                    a2a_rsem.at[ph, g],
                    {"expert": lax.rem(me + k, n)},
                ).start()

        arrived[ph, 0] = outgoing[ph, 0]

    dispatch(0, xs_finish(0))
    dispatch(1, xs_finish(1))

    def a2a_wait(ph, buf, g):
        @pl.when(g == 0)
        def _():
            pltpu.make_async_copy(buf.at[1:G], buf.at[1:G], a2a_rsem.at[ph, 0]).wait()

        @pl.when(g != 0)
        def _():
            ks = pl.ds(pl.multiple_of(g * G, G), G)
            pltpu.make_async_copy(buf.at[ks], buf.at[ks], a2a_rsem.at[ph, g]).wait()

    def group_rows(g):
        return pl.ds(pl.multiple_of(g * RG, RG), RG)

    halves = (slice(0, W), slice(W, 2 * W))

    def ag_copy(ph, g, kind, q):
        src = full.at[ph, q, group_rows(g)]
        if kind >= 2:
            src = full.at[ph, q, group_rows(g), halves[kind - 2]]
        where = {"dp": right if kind % 2 == 0 else left}
        return remote(src, src, ag_ssem.at[ph, g, kind], ag_rsem.at[ph, g, kind], where)

    def ag_start(ph, g):
        a2a_wait(ph, arrived.at[ph], g)
        for sub in range(G // 4):
            ks = pl.ds(pl.multiple_of(g * G + sub * 4, 4), 4)
            block = arrived[ph, ks].astype(F32).reshape(4 * R2, W).astype(BF16)
            dense = jnp.dot(perm[1], block, preferred_element_type=F32).astype(BF16)
            rows = pl.ds(pl.multiple_of(g * RG + sub * 4 * R, 4 * R), 4 * R)
            full[ph, x, rows, 0:W] = dense[: 4 * R]
            full[ph, x, rows, W : 2 * W] = dense[4 * R :]
        ag_copy(ph, g, 0, x).start()
        ag_copy(ph, g, 1, x).start()

    def ag_forward(ph, g):
        ag_copy(ph, g, 0, left).wait_recv()
        ag_copy(ph, g, 2, left).start()
        ag_copy(ph, g, 1, right).wait_recv()
        ag_copy(ph, g, 3, right).start()

    def ag_finish(ph, g):
        ag_copy(ph, g, 2, opp).wait_recv()
        ag_copy(ph, g, 3, opp).wait_recv()

    def chunk_rows(c):
        return pl.ds(pl.multiple_of(c * RC, RC), RC)

    def rs_copy(ph, c, kind):
        rows = chunk_rows(c)
        src, dst, where = (
            (part.at[ph, opp, rows, halves[0]], relay.at[ph, 0, rows], left),
            (part.at[ph, opp, rows, halves[1]], relay.at[ph, 1, rows], right),
            (part.at[ph, left, rows, halves[1]], frm.at[ph, 1, rows, halves[1]], left),
            (part.at[ph, right, rows, halves[0]], frm.at[ph, 0, rows, halves[0]], right),
            (part.at[ph, left, rows, halves[0]], frm.at[ph, 1, rows, halves[0]], left),
            (part.at[ph, right, rows, halves[1]], frm.at[ph, 0, rows, halves[1]], right),
        )[kind]
        return remote(src, dst, rs_ssem.at[ph, c, kind], rs_rsem.at[ph, c, kind], {"dp": where})

    def rs_start(ph, c, value):
        for j in range(4):
            part[ph, j, chunk_rows(c)] = value[:, j * Q : (j + 1) * Q].astype(BF16)
        for kind in range(4):
            rs_copy(ph, c, kind).start()

    def rs_relay(ph, c):
        rows = chunk_rows(c)
        for kind, target in ((0, left), (1, right)):
            rs_copy(ph, c, kind).wait_recv()
            own = part[ph, target, rows, halves[kind]].astype(F32)
            part[ph, target, rows, halves[kind]] = (own + relay[ph, kind, rows].astype(F32)).astype(BF16)
            rs_copy(ph, c, 4 + kind).start()

    def rs_finish(ph, c):
        for kind in (2, 3, 4, 5):
            rs_copy(ph, c, kind).wait_recv()

        @pl.loop(0, GC * G // 4)
        def _(sub):
            base = c * (GC * G) + sub * 4
            rows = pl.ds(pl.multiple_of(base * R, 4 * R), 4 * R)
            total = part[ph, x, rows].astype(F32) + frm[ph, 0, rows].astype(F32) + frm[ph, 1, rows].astype(F32)
            total = total.astype(BF16)
            stacked = jnp.concatenate([total[:, :W], total[:, W:]], axis=0)
            block = jnp.dot(perm[0], stacked, preferred_element_type=F32)
            leaving[ph, pl.ds(pl.multiple_of(base, 4), 4)] = block.reshape(4, R2, W).astype(BF16)

            @pl.loop(jnp.maximum(base, 1), base + 4)
            def _(k):
                remote(
                    leaving.at[ph, k],
                    returned.at[ph, k],
                    a2a_ssem.at[2 + ph],
                    a2a_rsem.at[2 + ph, lax.div(k, G)],
                    {"expert": lax.rem(me + n - k, n)},
                ).start()

    def fwd(c):
        rows = chunk_rows(c)
        block = jnp.concatenate([full[0, j, rows] for j in range(4)], axis=1)
        pre_gate = jnp.dot(block, gate_v[...], preferred_element_type=F32)
        pre_up = jnp.dot(block, up_v[...], preferred_element_type=F32)
        pg_v[rows, :] = pre_gate
        pu_v[rows, :] = pre_up
        hidden = (pre_gate * jax.nn.sigmoid(pre_gate) * pre_up).astype(BF16)
        hid_v[rows, :] = hidden
        return jnp.dot(hidden, down_v[...], preferred_element_type=F32)

    def bwd(c):
        rows = chunk_rows(c)
        block = jnp.concatenate([full[1, j, rows] for j in range(4)], axis=1)
        grad_hidden = lax.dot_general(block, down_v[...], LAST, preferred_element_type=F32)
        pre_gate = pg_v[rows, :]
        pre_up = pu_v[rows, :]
        s = jax.nn.sigmoid(pre_gate)
        grad_gate = (grad_hidden * pre_up * (s * (1.0 + pre_gate * (1.0 - s)))).astype(BF16)
        grad_up = (grad_hidden * (pre_gate * s)).astype(BF16)
        gpg_v[rows, :] = grad_gate
        gpu_v[rows, :] = grad_up
        value = lax.dot_general(grad_gate, gate_v[...], LAST, preferred_element_type=F32)
        return value + lax.dot_general(grad_up, up_v[...], LAST, preferred_element_type=F32)

    @pl.loop(0, NG)
    def _(g):
        ag_start(0, g)

        @pl.when(g > 0)
        def _():
            ag_forward(0, g - 1)

    ag_forward(0, NG - 1)
    for load in loads[4:]:
        load.wait()

    @pl.loop(0, NC)
    def _(c):
        for i in range(GC):
            g = c * GC + i
            ag_start(1, g)

            @pl.when(g > 0)
            def _():
                ag_forward(1, g - 1)

        for i in range(GC):
            ag_finish(0, c * GC + i)
        rs_start(0, c, fwd(c))

        @pl.when(c > 0)
        def _():
            rs_relay(0, c - 1)

    ag_forward(1, NG - 1)
    rs_relay(0, NC - 1)

    @pl.loop(0, NC)
    def _(c):
        for i in range(GC):
            ag_finish(1, c * GC + i)
        rs_start(1, c, bwd(c))
        rs_finish(0, c)

        @pl.when(c > 0)
        def _():
            rs_relay(1, c - 1)

    rs_relay(1, NC - 1)
    returned[0, 0] = leaving[0, 0]

    @pl.loop(0, NC)
    def _(c):
        rs_finish(1, c)

    returned[1, 0] = leaving[1, 0]

    def combine(ph, weights):
        total = jnp.zeros((2 * T, W), F32)

        def step(g, total):
            a2a_wait(2 + ph, returned.at[ph], g)
            ks = pl.ds(pl.multiple_of(g * G, G), G)
            rows = pl.ds(pl.multiple_of(g * G * R2, G * R2), G * R2)
            block = returned[ph, ks].astype(F32).reshape(G * R2, W).astype(BF16)
            for weight in weights:
                total = total + lax.dot_general(weight[rows, :], block, FIRST, preferred_element_type=F32)
            return total

        total = lax.fori_loop(0, NG, step, total)
        return jnp.concatenate([total[:T], total[T:]], axis=1).astype(BF16)

    def lanes_of(q):
        return pl.ds(pl.multiple_of(q * Q, Q), Q)

    def fin_copy(ph, q, peer, slot):
        src = lat_v.at[ph, core, :, lanes_of(q)]
        return remote(src, src, fin_ssem.at[ph, peer], fin_rsem.at[ph, slot], {"dp": peer})

    def fin_sib(ph, q, whose):
        src = lat_v.at[ph, whose, :, lanes_of(q)]
        return remote(src, src, sib_ssem.at[2 + 4 * ph + q], sib_rsem.at[2 + 4 * ph + q], sibling)

    def fin_start(ph, value):
        lat_v[ph, core, :, lanes_of(x)] = value
        for peer in peers:
            fin_copy(ph, x, peer, x).start()
        fin_sib(ph, x, core).start()

    def fin_finish(ph):
        for peer in peers:
            fin_copy(ph, peer, peer, peer).wait_recv()
            fin_sib(ph, peer, core).start()

    cols = Dd // 2

    def col_chunk(c):
        return slice(c * cols, (c + 1) * cols)

    def ring_copy(ph, c, kind):
        base = c * cols
        parts = (slice(base, base + cols // 2), slice(base + cols // 2, base + cols))
        src, dst, where = (
            (gpart.at[ph, y_opp, :, parts[0]], grelay.at[ph, c, 0], y_left),
            (gpart.at[ph, y_opp, :, parts[1]], grelay.at[ph, c, 1], y_right),
            (gpart.at[ph, y_left, :, parts[1]], gfrm.at[ph, 1, :, parts[1]], y_left),
            (gpart.at[ph, y_right, :, parts[0]], gfrm.at[ph, 0, :, parts[0]], y_right),
            (gpart.at[ph, y_left, :, parts[0]], gfrm.at[ph, 1, :, parts[0]], y_left),
            (gpart.at[ph, y_right, :, parts[1]], gfrm.at[ph, 0, :, parts[1]], y_right),
        )[kind]
        return remote(src, dst, ring_ssem.at[ph, c, kind], ring_rsem.at[ph, c, kind], at_y(where))

    def ring_start(ph):
        if ph == 0:
            sib_copy(1).wait_recv()
        else:
            sib_copy(0).wait_recv()
        for q in range(4):
            fin_sib(ph, q, 1 - core).wait_recv()
        other = (go_v, tok_v)[ph]
        chosen = jnp.dot(lat_v[ph].reshape(2 * T, L), sel_v[...], preferred_element_type=F32).astype(BF16)
        for c in range(2):
            right_side = other[:, :, col_chunk(c)].reshape(2 * T, cols)
            value = lax.dot_general(chosen, right_side, FIRST, preferred_element_type=F32).astype(BF16)
            gpart[ph, :, :, col_chunk(c)] = value.reshape(4, Z * RB, cols)
            for kind in range(4):
                ring_copy(ph, c, kind).start()

    def ring_relay(ph):
        for c in range(2):
            base = c * cols
            parts = (slice(base, base + cols // 2), slice(base + cols // 2, base + cols))
            for kind, target in ((0, y_left), (1, y_right)):
                ring_copy(ph, c, kind).wait_recv()
                own = gpart[ph, target, :, parts[kind]].astype(F32)
                gpart[ph, target, :, parts[kind]] = (own + grelay[ph, c, kind].astype(F32)).astype(BF16)
                ring_copy(ph, c, 4 + kind).start()

    def z_copy(ph, c, step, source, target):
        return remote(
            zsend.at[ph, target, :, col_chunk(c)],
            zrecv.at[ph, source, :, col_chunk(c)],
            z_ssem.at[ph, c, step],
            z_rsem.at[ph, c, step],
            {"expert": (target * 4 + y) * 2 + core},
        )

    def ring_finish(ph):
        for c in range(2):
            for kind in (2, 3, 4, 5):
                ring_copy(ph, c, kind).wait_recv()
            here = col_chunk(c)
            total = gpart[ph, y, :, here].astype(F32) + gfrm[ph, 0, :, here].astype(F32) + gfrm[ph, 1, :, here].astype(F32)
            total = total.reshape(Z, RB, cols)
            gsum[ph, :, :, here] = total
            zsend[ph, :, :, here] = total.astype(BF16)
            for step in range(1, Z):
                z_copy(ph, c, step, z, lax.rem(z + step, Z)).start()

    def z_finish(ph):
        for c in range(2):
            here = col_chunk(c)
            total = gsum[ph, z, :, here]
            for step in range(1, Z):
                source = lax.rem(z + Z - step, Z)
                z_copy(ph, c, step, source, z).wait_recv()
                total = total + zrecv[ph, source, :, here].astype(F32)
            gsum[ph, z, :, here] = total * scaling
        store(gsum.at[ph, z], (gfl_out, gtl_out)[ph])

    stores = []

    def store(src, dst):
        copy = pltpu.make_async_copy(src, dst, store_sem.at[len(stores)])
        copy.start()
        stores.append(copy)

    fin_start(0, combine(0, (pph, ppl)))

    @pl.loop(0, 4)
    def _(j):
        rows = pl.ds(pl.multiple_of(j * Q, Q), Q)
        block = full[0, j]
        gg_v[rows, :] = (lax.dot_general(block, gpg_v[...], FIRST, preferred_element_type=F32) * scaling).astype(BF16)
        gu_v[rows, :] = (lax.dot_general(block, gpu_v[...], FIRST, preferred_element_type=F32) * scaling).astype(BF16)

    store(gg_v, gg_out.at[0])
    store(gu_v, gu_out.at[0])
    fin_finish(0)
    lo_v[...] = jnp.dot(lat_v[0, core], fl_v[...], preferred_element_type=F32).astype(BF16)
    store(lo_v, lo_out)
    ring_start(0)

    @pl.loop(0, 4)
    def _(j):
        rows = pl.ds(pl.multiple_of(j * Q, Q), Q)
        gd_v[:, rows] = (
            lax.dot_general(hid_v[...], full[1, j], FIRST, preferred_element_type=F32) * scaling
        ).astype(BF16)

    store(gd_v, gd_out.at[0])
    ring_relay(0)
    fin_start(1, combine(1, (pp,)))
    ring_finish(0)
    fin_finish(1)
    gt_v[...] = lax.dot_general(lat_v[1, core], tl_v[...], LAST, preferred_element_type=F32).astype(BF16)
    store(gt_v, gt_out)
    ring_start(1)
    z_finish(0)
    ring_relay(1)
    ring_finish(1)
    z_finish(1)

    for ph in range(2):
        for peer in peers:
            xs_copy(ph, peer).wait_send()
        sib_copy(ph).wait_send()
        for peer in peers:
            fin_copy(ph, x, peer, x).wait_send()
        for q in range(4):
            fin_sib(ph, q, core).wait_send()
        for c in range(2):
            for kind in range(6):
                ring_copy(ph, c, kind).wait_send()
            for step in range(1, Z):
                z_copy(ph, c, step, z, lax.rem(z + step, Z)).wait_send()
        for buf, sem in ((outgoing.at[ph], a2a_ssem.at[ph]), (leaving.at[ph], a2a_ssem.at[2 + ph])):
            pltpu.make_async_copy(buf.at[1:n], buf.at[1:n], sem).wait()

        @pl.loop(0, NG)
        def _(g):
            for kind, q in ((0, x), (1, x), (2, left), (3, right)):
                ag_copy(ph, g, kind, q).wait_send()

        @pl.loop(0, NC)
        def _(c):
            for kind in range(6):
                rs_copy(ph, c, kind).wait_send()

    for copy in stores:
        copy.wait()


def layer_call(capacity, n, routes, slot_index, route_gates, tokens, to_latent, from_latent, gate, up, down, grad_output):
    T, Dd = tokens.shape
    L = to_latent.shape[1]
    Hs = gate.shape[2]
    Q, W = L // 4, L // 8
    R = capacity
    G = 8 if n >= 16 else 4
    NG = n // G
    NC = min(4, NG)
    Z, RB = n // 8, L // n
    cfg = dict(Z=Z, RB=RB, Dd=Dd, n=n, T=T, R=R, L=L, Q=Q, W=W, G=G, NG=NG, NC=NC, scaling=float((T * n) ** -0.5))
    rows = n * R
    vm = lambda shape, dtype=BF16: pltpu.VMEM(shape, dtype)
    dma = lambda *shape: pltpu.SemaphoreType.DMA(shape)
    any_spec = pl.BlockSpec(memory_space=pl.ANY)
    vm_spec = pl.BlockSpec(memory_space=pltpu.VMEM)
    outs = [
        ((T, Dd), BF16),
        ((T, Dd), BF16),
        (gate.shape, BF16),
        (up.shape, BF16),
        (down.shape, BF16),
        ((RB, Dd), F32),
        ((RB, Dd), F32),
    ]
    scratch = [
        vm((2, T, Dd)),
        vm((Dd, L)),
        vm((L, Dd)),
        vm((L, Hs)),
        vm((L, Hs)),
        vm((Hs, L)),
        vm((2, T, Dd)),
        vm((T, Dd)),
        vm((T, Dd)),
        vm((L, Hs)),
        vm((L, Hs)),
        vm((Hs, L)),
        vm((2, 2, T, L)),
        vm((L, L // 2)),
        vm((2, 4, Z * RB, Dd)),
        vm((2, 2, 2, Z * RB, Dd // 4)),
        vm((2, 2, Z * RB, Dd)),
        vm((2, Z, RB, Dd)),
        vm((2, Z, RB, Dd)),
        vm((2, Z, RB, Dd), F32),
        vm((2, 4, T, Q)),
        vm((2, 4, T, Q)),
        vm((n, T), jnp.int32),
        vm((n, T), F32),
        vm((2 * rows, 2 * T)),
        vm((2 * rows, 2 * T)),
        vm((2 * rows, 2 * T)),
        vm((2, 8 * R, 8 * R)),
        vm((2, n, 2 * R, W)),
        vm((2, n, 2 * R, W)),
        vm((2, n, 2 * R, W)),
        vm((2, n, 2 * R, W)),
        vm((2, 4, rows, Q)),
        vm((2, 4, rows, Q)),
        vm((2, 2, rows, W)),
        vm((2, 2, rows, Q)),
        vm((rows, Hs), F32),
        vm((rows, Hs), F32),
        vm((rows, Hs)),
        vm((rows, Hs)),
        vm((rows, Hs)),
        dma(7),
        dma(7),
        dma(2, 4),
        dma(2, 4),
        dma(4),
        dma(4, NG),
        dma(2, NG, 4),
        dma(2, NG, 4),
        dma(2, NC, 6),
        dma(2, NC, 6),
        dma(2, 4),
        dma(2, 4),
        dma(10),
        dma(10),
        dma(2, 2, 6),
        dma(2, 2, 6),
        dma(2, 2, Z),
        dma(2, 2, Z),
    ]
    flops = 2 * rows * L * Hs * 9 + 2 * T * L * Dd * 4
    return pl.pallas_call(
        functools.partial(layer_kernel, cfg),
        out_shape=[jax.ShapeDtypeStruct(s, d) for s, d in outs],
        in_specs=[vm_spec] * 3 + [any_spec] * 7,
        out_specs=[any_spec] * len(outs),
        scratch_shapes=scratch,
        compiler_params=pltpu.CompilerParams(
            collective_id=0, has_side_effects=True, vmem_limit_bytes=62 * 1024 * 1024
        ),
        cost_estimate=pl.CostEstimate(flops=flops, bytes_accessed=16 * 2**20, transcendentals=rows * Hs),
    )(routes.T, slot_index.T, route_gates.T, tokens, to_latent, from_latent, gate, up, down, grad_output)


def local(
    tokens,
    to_latent,
    from_latent,
    expert_gate,
    expert_up,
    expert_down,
    routes,
    slot_index,
    route_gates,
    grad_output,
):
    expert_count = lax.axis_size("expert")
    dp_count = lax.axis_size("dp")
    token_count, route_count = routes.shape
    capacity = dp_count * max(
        1,
        min(
            token_count // (4 * dp_count),
            5 * token_count * route_count // (4 * expert_count * dp_count),
        ),
    )
    (layer_output, grad_tokens, grad_gate, grad_up, grad_down, grad_to_latent, grad_from_latent) = layer_call(
        capacity,
        expert_count,
        routes,
        slot_index,
        route_gates,
        tokens,
        to_latent,
        from_latent,
        expert_gate,
        expert_up,
        expert_down,
        grad_output,
    )
    return (
        layer_output,
        grad_tokens,
        grad_to_latent,
        grad_from_latent,
        grad_gate,
        grad_up,
        grad_down,
    )


def solution(mesh):
    return jax.shard_map(
        local,
        mesh=mesh,
        in_specs=(
            P("expert", "dp"),
            P("dp", None),
            P(None, "dp"),
            P("expert", None, "dp"),
            P("expert", None, "dp"),
            P("expert", "dp", None),
            P("expert", None),
            P("expert", None),
            P("expert", None),
            P("expert", "dp"),
        ),
        out_specs=(
            P("expert", "dp"),
            P("expert", "dp"),
            P("expert", "dp"),
            P("expert", "dp"),
            P("expert", None, "dp"),
            P("expert", None, "dp"),
            P("expert", "dp", None),
        ),
        check_vma=False,
    )
```

```python
import functools

import jax
import jax.numpy as jnp
from jax import lax
from jax.experimental import pallas as pl
from jax.experimental.pallas import tpu as pltpu
from jax.sharding import PartitionSpec as P

F32 = jnp.float32
BF16 = jnp.bfloat16
LAST = (((1,), (1,)), ((), ()))
FIRST = (((0,), (0,)), ((), ()))
MESH = pl.DeviceIdType.MESH


def remote(src, dst, send_sem, recv_sem, where):
    return pltpu.make_async_remote_copy(
        src_ref=src, dst_ref=dst, send_sem=send_sem, recv_sem=recv_sem, device_id=where, device_id_type=MESH
    )


def layer_kernel(
    cfg,
    routes_ref,
    slots_ref,
    gates_ref,
    tok_in,
    tl_in,
    fl_in,
    gate_in,
    up_in,
    down_in,
    go_in,
    lo_out,
    gt_out,
    gg_out,
    gu_out,
    gd_out,
    gtl_out,
    gfl_out,
    tok_g,
    tl_v,
    fl_v,
    gate_v,
    up_v,
    down_v,
    go_g,
    lo_v,
    gt_v,
    gg_v,
    gu_v,
    gd_v,
    lat_v,
    turned,
    taken,
    zsend,
    zrecv,
    gsum,
    xs_send_v,
    xs_recv_v,
    s_tab,
    g_tab,
    pp,
    pph,
    ppl,
    perm,
    outgoing,
    arrived,
    leaving,
    returned,
    full,
    part,
    relay,
    frm,
    pg_v,
    pu_v,
    hid_v,
    gpg_v,
    gpu_v,
    load_sem,
    store_sem,
    xs_ssem,
    xs_rsem,
    a2a_ssem,
    a2a_rsem,
    ag_ssem,
    ag_rsem,
    rs_ssem,
    rs_rsem,
    fin_ssem,
    fin_rsem,
    sib_ssem,
    sib_rsem,
    near_ssem,
    near_rsem,
    turn_ssem,
    turn_rsem,
    z_ssem,
    z_rsem,
    y_ready,
    core_ready,
):
    Z, Y, RB, Dd = cfg["Z"], cfg["Y"], cfg["RB"], cfg["Dd"]
    U = 2 * Y
    n, T, R, L, Q, W, G, NG, NC = (cfg[k] for k in ("n", "T", "R", "L", "Q", "W", "G", "NG", "NC"))
    scaling = cfg["scaling"]
    R2 = 2 * R
    RG = G * R
    RC = n * R // NC
    GC = NG // NC
    me = lax.axis_index("expert")
    x = lax.axis_index("dp")
    right = lax.rem(x + 1, 4)
    left = lax.rem(x + 3, 4)
    opp = lax.rem(x + 2, 4)
    peers = (right, left, opp)
    core = lax.rem(me, 2)
    y = lax.rem(lax.div(me, 2), Y)
    z = lax.div(me, 2 * Y)
    unit = y * 2 + core

    def at(zz, yy, cc):
        return (zz * Y + yy) * 2 + cc

    sibling = {"expert": at(z, y, 1 - core)}

    def offsets(i):
        j = i & (Z - 1)
        u = lax.shift_right_logical(i, Z.bit_length() - 1)
        step = lax.shift_right_logical(j + 1, 1)
        dz = jnp.where((j & 1) == 1, step, Z - step)
        return dz, lax.shift_right_logical(u, 1), u & 1

    def target_of(i):
        dz, dy, dc = offsets(i)
        return at((z + dz) & (Z - 1), (y + dy) & (Y - 1), (core + dc) & 1)

    def source_of(i):
        dz, dy, dc = offsets(i)
        return at((z + 2 * Z - dz) & (Z - 1), (y + Y - dy) & (Y - 1), (core + dc) & 1)

    loads = [
        pltpu.make_async_copy(src, dst, load_sem.at[i])
        for i, (src, dst) in enumerate(
            (
                (tok_in, tok_g.at[0]),
                (tl_in, tl_v),
                (go_in, go_g.at[0]),
                (fl_in, fl_v),
                (gate_in.at[0], gate_v),
                (up_in.at[0], up_v),
                (down_in.at[0], down_v),
            )
        )
    ]
    for load in loads[:2]:
        load.start()

    def signal(sem, where):
        pl.semaphore_signal(sem, inc=1, device_id=where, device_id_type=MESH)

    barrier = pltpu.get_barrier_semaphore()
    for peer in peers:
        signal(barrier, {"dp": peer})
    signal(barrier, sibling)
    for step in range(1, Y):
        signal(barrier, {"expert": at(z, (y + step) & (Y - 1), core)})
    for step in range(1, Z):
        signal(barrier, {"expert": at((z + step) & (Z - 1), y, core)})
    near_count = 3 + 1 + (Y - 1) + (Z - 1)

    whose = target_of(lax.broadcasted_iota(jnp.int32, (n, T), 0))
    s_val = jnp.full((n, T), -1000, jnp.int32)
    g_val = jnp.zeros((n, T), F32)
    for j in range(routes_ref.shape[0]):
        slot = slots_ref[j : j + 1, :]
        match = (whose == routes_ref[j : j + 1, :]) & (slot < R)
        s_val = jnp.where(match, slot, s_val)
        g_val = jnp.where(match, gates_ref[j : j + 1, :], g_val)
    s_tab[...] = s_val
    g_tab[...] = g_val

    size = 4 * R2
    row = lax.broadcasted_iota(jnp.int32, (size, size), 0)
    col = lax.broadcasted_iota(jnp.int32, (size, size), 1)
    kk = jnp.where(row >= 2 * R2, jnp.where(row >= 3 * R2, 3, 2), jnp.where(row >= R2, 1, 0))
    rest = row - kk * R2
    half = jnp.where(rest >= R, 1, 0)
    perm[0] = jnp.where(col == half * (4 * R) + kk * R + rest - half * R, 1.0, 0.0).astype(BF16)
    kk = jnp.where(col >= 2 * R2, jnp.where(col >= 3 * R2, 3, 2), jnp.where(col >= R2, 1, 0))
    rest = col - kk * R2
    half = jnp.where(rest >= R, 1, 0)
    perm[1] = jnp.where(row == half * (4 * R) + kk * R + rest - half * R, 1.0, 0.0).astype(BF16)

    def xs_copy(ph, j):
        return remote(
            xs_send_v.at[ph, j], xs_recv_v.at[ph, x], xs_ssem.at[ph, j], xs_rsem.at[ph, x], {"dp": j}
        )

    def xs_start(ph, value):
        for j in range(4):
            xs_send_v[ph, j] = value[:, j * Q : (j + 1) * Q].astype(BF16)
        for peer in peers:
            xs_copy(ph, peer).start()

    def xs_finish(ph):
        total = xs_send_v[ph, x].astype(F32)
        for peer in peers:
            remote(
                xs_send_v.at[ph, x], xs_recv_v.at[ph, peer], xs_ssem.at[ph, peer], xs_rsem.at[ph, peer], {"dp": peer}
            ).wait_recv()
            total = total + xs_recv_v[ph, peer].astype(F32)
        total = total.astype(BF16)
        return jnp.concatenate([total[:, :W], total[:, W:]], axis=0)

    loads[0].wait()
    loads[1].wait()
    loads[2].start()
    loads[3].start()
    latent_part = jnp.dot(tok_g[0], tl_v[...], preferred_element_type=F32)
    pl.semaphore_wait(barrier, near_count)
    xs_start(0, latent_part)
    for step in range(1, Y):
        signal(y_ready, {"expert": at(z, (y + step) & (Y - 1), core)})
    loads[2].wait()
    loads[3].wait()
    for load in loads[4:]:
        load.start()
    xs_start(1, lax.dot_general(go_g[0], fl_v[...], LAST, preferred_element_type=F32))
    if Y > 1:
        pl.semaphore_wait(y_ready, Y - 1)
    signal(core_ready, sibling)

    r_iota = lax.broadcasted_iota(jnp.int32, (G, R2, T), 1)

    @pl.loop(0, NG)
    def _(g):
        ks = pl.ds(pl.multiple_of(g * G, G), G)
        rows = pl.ds(pl.multiple_of(g * G * R2, G * R2), G * R2)
        s8 = jnp.broadcast_to(s_tab[ks, :].reshape(G, 1, T), (G, R2, T))
        g8 = jnp.broadcast_to(g_tab[ks, :].reshape(G, 1, T), (G, R2, T))
        g_hi = g8.astype(BF16).astype(F32)
        g_lo = g8 - g_hi
        for h in range(2):
            match = s8 == r_iota - h * R
            lanes = slice(h * T, (h + 1) * T)
            pp[rows, lanes] = jnp.where(match, 1.0, 0.0).reshape(G * R2, T).astype(BF16)
            pph[rows, lanes] = jnp.where(match, g_hi, 0.0).reshape(G * R2, T).astype(BF16)
            ppl[rows, lanes] = jnp.where(match, g_lo, 0.0).reshape(G * R2, T).astype(BF16)

    def dispatch(ph, stacked):
        @pl.loop(0, NG)
        def _(g):
            ks = pl.ds(pl.multiple_of(g * G, G), G)
            rows = pl.ds(pl.multiple_of(g * G * R2, G * R2), G * R2)
            if ph == 0:
                block = jnp.dot(pp[rows, :], stacked, preferred_element_type=F32)
            else:
                block = jnp.dot(pph[rows, :], stacked, preferred_element_type=F32)
                block = block + jnp.dot(ppl[rows, :], stacked, preferred_element_type=F32)
            outgoing[ph, ks] = block.reshape(G, R2, W).astype(BF16)

            @pl.loop(jnp.maximum(g * G, 1), g * G + G)
            def _(k):
                remote(
                    outgoing.at[ph, k],
                    arrived.at[ph, k],
                    a2a_ssem.at[ph],
                    a2a_rsem.at[ph, g],
                    {"expert": target_of(k)},
                ).start()

        arrived[ph, 0] = outgoing[ph, 0]

    latent_rows = xs_finish(0)
    pl.semaphore_wait(core_ready, 1)
    dispatch(0, latent_rows)
    dispatch(1, xs_finish(1))

    def sib_copy(i, dy):
        ref = (tok_g, go_g)[i]
        dst = ref.at[(2 * dy + 1 - 2 * core + U) & (U - 1)]
        return remote(ref.at[2 * dy], dst, sib_ssem.at[i, dy], sib_rsem.at[i, dy], sibling)

    def sib_wait(i, dy):
        ref = (tok_g, go_g)[i]
        here = (2 * dy + 2 * core - 1 + U) & (U - 1)
        remote(ref.at[2 * dy], ref.at[here], sib_ssem.at[i, dy], sib_rsem.at[i, dy], sibling).wait_recv()

    def near_copy(i, dy):
        ref = (tok_g, go_g)[i]
        return remote(
            ref.at[0],
            ref.at[2 * dy],
            near_ssem.at[i, dy],
            near_rsem.at[i, dy],
            {"expert": at(z, (y + dy) & (Y - 1), core)},
        )

    def near_start(i):
        sib_copy(i, 0).start()
        for dy in range(1, Y):
            near_copy(i, dy).start()

    def near_forward(i):
        for dy in range(1, Y):
            near_copy(i, dy).wait_recv()
            sib_copy(i, dy).start()

    def near_finish(i):
        for dy in range(Y):
            sib_wait(i, dy)

    near_start(1)
    near_start(0)

    def a2a_wait(ph, buf, g):
        @pl.when(g == 0)
        def _():
            pltpu.make_async_copy(buf.at[1:G], buf.at[1:G], a2a_rsem.at[ph, 0]).wait()

        @pl.when(g != 0)
        def _():
            ks = pl.ds(pl.multiple_of(g * G, G), G)
            pltpu.make_async_copy(buf.at[ks], buf.at[ks], a2a_rsem.at[ph, g]).wait()

    def group_rows(g):
        return pl.ds(pl.multiple_of(g * RG, RG), RG)

    halves = (slice(0, W), slice(W, 2 * W))

    def ag_copy(ph, g, kind, q):
        src = full.at[ph, q, group_rows(g)]
        if kind >= 2:
            src = full.at[ph, q, group_rows(g), halves[kind - 2]]
        where = {"dp": right if kind % 2 == 0 else left}
        return remote(src, src, ag_ssem.at[ph, g, kind], ag_rsem.at[ph, g, kind], where)

    def ag_start(ph, g):
        a2a_wait(ph, arrived.at[ph], g)
        for sub in range(G // 4):
            ks = pl.ds(pl.multiple_of(g * G + sub * 4, 4), 4)
            block = arrived[ph, ks].astype(F32).reshape(4 * R2, W).astype(BF16)
            dense = jnp.dot(perm[1], block, preferred_element_type=F32).astype(BF16)
            rows = pl.ds(pl.multiple_of(g * RG + sub * 4 * R, 4 * R), 4 * R)
            full[ph, x, rows, 0:W] = dense[: 4 * R]
            full[ph, x, rows, W : 2 * W] = dense[4 * R :]
        ag_copy(ph, g, 0, x).start()
        ag_copy(ph, g, 1, x).start()

    def ag_forward(ph, g):
        ag_copy(ph, g, 0, left).wait_recv()
        ag_copy(ph, g, 2, left).start()
        ag_copy(ph, g, 1, right).wait_recv()
        ag_copy(ph, g, 3, right).start()

    def ag_finish(ph, g):
        ag_copy(ph, g, 2, opp).wait_recv()
        ag_copy(ph, g, 3, opp).wait_recv()

    def chunk_rows(c):
        return pl.ds(pl.multiple_of(c * RC, RC), RC)

    def rs_copy(ph, c, kind):
        rows = chunk_rows(c)
        src, dst, where = (
            (part.at[ph, opp, rows, halves[0]], relay.at[ph, 0, rows], left),
            (part.at[ph, opp, rows, halves[1]], relay.at[ph, 1, rows], right),
            (part.at[ph, left, rows, halves[1]], frm.at[ph, 1, rows, halves[1]], left),
            (part.at[ph, right, rows, halves[0]], frm.at[ph, 0, rows, halves[0]], right),
            (part.at[ph, left, rows, halves[0]], frm.at[ph, 1, rows, halves[0]], left),
            (part.at[ph, right, rows, halves[1]], frm.at[ph, 0, rows, halves[1]], right),
        )[kind]
        return remote(src, dst, rs_ssem.at[ph, c, kind], rs_rsem.at[ph, c, kind], {"dp": where})

    def rs_start(ph, c, value):
        for j in range(4):
            part[ph, j, chunk_rows(c)] = value[:, j * Q : (j + 1) * Q].astype(BF16)
        for kind in range(4):
            rs_copy(ph, c, kind).start()

    def rs_relay(ph, c):
        rows = chunk_rows(c)
        for kind, target in ((0, left), (1, right)):
            rs_copy(ph, c, kind).wait_recv()
            own = part[ph, target, rows, halves[kind]].astype(F32)
            part[ph, target, rows, halves[kind]] = (own + relay[ph, kind, rows].astype(F32)).astype(BF16)
            rs_copy(ph, c, 4 + kind).start()

    def rs_finish(ph, c):
        for kind in (2, 3, 4, 5):
            rs_copy(ph, c, kind).wait_recv()

        @pl.loop(0, GC * G // 4)
        def _(sub):
            base = c * (GC * G) + sub * 4
            rows = pl.ds(pl.multiple_of(base * R, 4 * R), 4 * R)
            total = part[ph, x, rows].astype(F32) + frm[ph, 0, rows].astype(F32) + frm[ph, 1, rows].astype(F32)
            total = total.astype(BF16)
            stacked = jnp.concatenate([total[:, :W], total[:, W:]], axis=0)
            block = jnp.dot(perm[0], stacked, preferred_element_type=F32)
            leaving[ph, pl.ds(pl.multiple_of(base, 4), 4)] = block.reshape(4, R2, W).astype(BF16)

            @pl.loop(jnp.maximum(base, 1), base + 4)
            def _(k):
                remote(
                    leaving.at[ph, k],
                    returned.at[ph, k],
                    a2a_ssem.at[2 + ph],
                    a2a_rsem.at[2 + ph, lax.div(k, G)],
                    {"expert": source_of(k)},
                ).start()

    def fwd(c):
        rows = chunk_rows(c)
        block = jnp.concatenate([full[0, j, rows] for j in range(4)], axis=1)
        pre_gate = jnp.dot(block, gate_v[...], preferred_element_type=F32)
        pre_up = jnp.dot(block, up_v[...], preferred_element_type=F32)
        pg_v[rows, :] = pre_gate
        pu_v[rows, :] = pre_up
        hidden = (pre_gate * jax.nn.sigmoid(pre_gate) * pre_up).astype(BF16)
        hid_v[rows, :] = hidden
        return jnp.dot(hidden, down_v[...], preferred_element_type=F32)

    def bwd(c):
        rows = chunk_rows(c)
        block = jnp.concatenate([full[1, j, rows] for j in range(4)], axis=1)
        grad_hidden = lax.dot_general(block, down_v[...], LAST, preferred_element_type=F32)
        pre_gate = pg_v[rows, :]
        pre_up = pu_v[rows, :]
        s = jax.nn.sigmoid(pre_gate)
        grad_gate = (grad_hidden * pre_up * (s * (1.0 + pre_gate * (1.0 - s)))).astype(BF16)
        grad_up = (grad_hidden * (pre_gate * s)).astype(BF16)
        gpg_v[rows, :] = grad_gate
        gpu_v[rows, :] = grad_up
        value = lax.dot_general(grad_gate, gate_v[...], LAST, preferred_element_type=F32)
        return value + lax.dot_general(grad_up, up_v[...], LAST, preferred_element_type=F32)

    @pl.loop(0, NG)
    def _(g):
        ag_start(0, g)

        @pl.when(g > 0)
        def _():
            ag_forward(0, g - 1)

    ag_forward(0, NG - 1)
    for load in loads[4:]:
        load.wait()

    @pl.loop(0, NC)
    def _(c):
        for i in range(GC):
            g = c * GC + i
            ag_start(1, g)

            @pl.when(g > 0)
            def _():
                ag_forward(1, g - 1)

        for i in range(GC):
            ag_finish(0, c * GC + i)
        rs_start(0, c, fwd(c))

        @pl.when(c > 0)
        def _():
            rs_relay(0, c - 1)

    ag_forward(1, NG - 1)
    rs_relay(0, NC - 1)

    @pl.loop(0, NC)
    def _(c):
        for i in range(GC):
            ag_finish(1, c * GC + i)
        rs_start(1, c, bwd(c))
        rs_finish(0, c)

        @pl.when(c > 0)
        def _():
            rs_relay(1, c - 1)

    rs_relay(1, NC - 1)
    returned[0, 0] = leaving[0, 0]

    @pl.loop(0, NC)
    def _(c):
        rs_finish(1, c)

    returned[1, 0] = leaving[1, 0]

    def combine(ph, weights):
        def step(g, total):
            a2a_wait(2 + ph, returned.at[ph], g)
            ks = pl.ds(pl.multiple_of(g * G, G), G)
            rows = pl.ds(pl.multiple_of(g * G * R2, G * R2), G * R2)
            block = returned[ph, ks].astype(F32).reshape(G * R2, W).astype(BF16)
            for weight in weights:
                total = total + lax.dot_general(block, weight[rows, :], FIRST, preferred_element_type=F32)
            return total

        total = lax.fori_loop(0, NG, step, jnp.zeros((W, 2 * T), F32))
        for h in range(2):
            turned[ph, :, h] = total[:, h * T : (h + 1) * T].reshape(U, RB, T).astype(BF16)
        taken[ph, 0] = turned[ph, unit]

        @pl.loop(1, 4 * U)
        def _(m):
            turn_copy(ph, m).start()

        lat_v[ph, :, lanes_of(x)] = jnp.concatenate([total[:, :T].T, total[:, T:].T], axis=1).astype(BF16)
        for peer in peers:
            fin_copy(ph, x, peer, x).start()

    def turn_copy(ph, m):
        dx = m & 3
        there = (unit + lax.shift_right_logical(m, 2)) & (U - 1)
        where = {"dp": (x + dx) & 3, "expert": z * U + there}
        return remote(turned.at[ph, there], taken.at[ph, m], turn_ssem.at[ph], turn_rsem.at[ph], where)

    def turn_wait(ph, sem, buf):
        pltpu.make_async_copy(buf.at[ph, 1 : 4 * U], buf.at[ph, 1 : 4 * U], sem.at[ph]).wait()

    def lanes_of(q):
        return pl.ds(pl.multiple_of(q * Q, Q), Q)

    def fin_copy(ph, q, peer, slot):
        src = lat_v.at[ph, :, lanes_of(q)]
        return remote(src, src, fin_ssem.at[ph, peer], fin_rsem.at[ph, slot], {"dp": peer})

    def fin_finish(ph):
        for peer in peers:
            fin_copy(ph, peer, peer, peer).wait_recv()

    cols = Dd // 2

    def col_chunk(c):
        return slice(c * cols, (c + 1) * cols)

    def z_copy(ph, c, step, source, target):
        return remote(
            zsend.at[ph, target, :, col_chunk(c)],
            zrecv.at[ph, source, :, col_chunk(c)],
            z_ssem.at[ph, c, step],
            z_rsem.at[ph, c, step],
            {"expert": at(target, y, core)},
        )

    def z_start(ph):
        near_finish(1 - ph)
        turn_wait(ph, turn_rsem, taken)
        other = (go_g, tok_g)[ph]
        left_side = jnp.concatenate(
            [taken[ph, 4 * u : 4 * u + 4].reshape(Z * RB, T) for u in range(U)], axis=1
        )
        for c in range(2):
            here = col_chunk(c)
            right_side = other[:, :, here].reshape(U * T, cols)
            value = jnp.dot(left_side, right_side, preferred_element_type=F32).reshape(4, 2, RB, cols)
            for dx in range(4):
                first = 2 * ((x + 4 - dx) & 3)
                gsum[ph, pl.ds(first, 2), :, here] = value[dx]
                zsend[ph, pl.ds(first, 2), :, here] = value[dx].astype(BF16)
            for step in range(1, Z):
                z_copy(ph, c, step, z, (z + step) & (Z - 1)).start()

    def z_finish(ph):
        for c in range(2):
            here = col_chunk(c)
            total = gsum[ph, z, :, here]
            for step in range(1, Z):
                source = (z + Z - step) & (Z - 1)
                z_copy(ph, c, step, source, z).wait_recv()
                total = total + zrecv[ph, source, :, here].astype(F32)
            gsum[ph, z, :, here] = total * scaling
        store(gsum.at[ph, z], (gfl_out, gtl_out)[ph])

    stores = []

    def store(src, dst):
        copy = pltpu.make_async_copy(src, dst, store_sem.at[len(stores)])
        copy.start()
        stores.append(copy)

    near_forward(1)
    combine(0, (pph, ppl))

    @pl.loop(0, 4)
    def _(j):
        rows = pl.ds(pl.multiple_of(j * Q, Q), Q)
        block = full[0, j]
        gg_v[rows, :] = (lax.dot_general(block, gpg_v[...], FIRST, preferred_element_type=F32) * scaling).astype(BF16)
        gu_v[rows, :] = (lax.dot_general(block, gpu_v[...], FIRST, preferred_element_type=F32) * scaling).astype(BF16)

    store(gg_v, gg_out.at[0])
    store(gu_v, gu_out.at[0])
    near_forward(0)
    fin_finish(0)
    lo_v[...] = jnp.dot(lat_v[0], fl_v[...], preferred_element_type=F32).astype(BF16)
    store(lo_v, lo_out)
    z_start(0)

    @pl.loop(0, 4)
    def _(j):
        rows = pl.ds(pl.multiple_of(j * Q, Q), Q)
        gd_v[:, rows] = (
            lax.dot_general(hid_v[...], full[1, j], FIRST, preferred_element_type=F32) * scaling
        ).astype(BF16)

    store(gd_v, gd_out.at[0])
    combine(1, (pp,))
    z_finish(0)
    z_start(1)
    fin_finish(1)
    gt_v[...] = lax.dot_general(lat_v[1], tl_v[...], LAST, preferred_element_type=F32).astype(BF16)
    store(gt_v, gt_out)
    z_finish(1)

    for ph in range(2):
        for peer in peers:
            xs_copy(ph, peer).wait_send()
        for dy in range(Y):
            sib_copy(ph, dy).wait_send()
        for dy in range(1, Y):
            near_copy(ph, dy).wait_send()
        for peer in peers:
            fin_copy(ph, x, peer, x).wait_send()
        turn_wait(ph, turn_ssem, taken)
        for c in range(2):
            for step in range(1, Z):
                z_copy(ph, c, step, z, (z + step) & (Z - 1)).wait_send()
        for buf, sem in ((outgoing.at[ph], a2a_ssem.at[ph]), (leaving.at[ph], a2a_ssem.at[2 + ph])):
            pltpu.make_async_copy(buf.at[1:n], buf.at[1:n], sem).wait()

        @pl.loop(0, NG)
        def _(g):
            for kind, q in ((0, x), (1, x), (2, left), (3, right)):
                ag_copy(ph, g, kind, q).wait_send()

        @pl.loop(0, NC)
        def _(c):
            for kind in range(6):
                rs_copy(ph, c, kind).wait_send()

    for copy in stores:
        copy.wait()


def copy_kernel(count, *refs):
    sources, targets, held = refs[:count], refs[count : 2 * count], refs[2 * count : 3 * count]
    into, out = refs[3 * count :]
    first = [pltpu.make_async_copy(sources[i], held[i], into.at[i]) for i in range(count)]
    second = [pltpu.make_async_copy(held[i], targets[i], out.at[i]) for i in range(count)]
    for copy in first:
        copy.start()
    for i in range(count):
        first[i].wait()
        second[i].start()
    for copy in second:
        copy.wait()


def copied(arrays):
    count = len(arrays)
    any_spec = pl.BlockSpec(memory_space=pl.ANY)
    return pl.pallas_call(
        functools.partial(copy_kernel, count),
        out_shape=[jax.ShapeDtypeStruct(a.shape, a.dtype) for a in arrays],
        in_specs=[any_spec] * count,
        out_specs=[any_spec] * count,
        scratch_shapes=[pltpu.VMEM(a.shape, a.dtype) for a in arrays] + [pltpu.SemaphoreType.DMA((count,))] * 2,
        compiler_params=pltpu.CompilerParams(vmem_limit_bytes=62 * 1024 * 1024),
        cost_estimate=pl.CostEstimate(flops=0, bytes_accessed=8 * 2**20, transcendentals=0),
    )(*arrays)


def layer_call(capacity, n, routes, slot_index, route_gates, tokens, to_latent, from_latent, gate, up, down, grad_output):
    T, Dd = tokens.shape
    L = to_latent.shape[1]
    Hs = gate.shape[2]
    Q, W = L // 4, L // 8
    R = capacity
    G = 8 if n >= 16 else 4
    NG = n // G
    NC = min(4, NG)
    Z, RB = 8, L // n
    Y = n // (2 * Z)
    U = 2 * Y
    cfg = dict(Z=Z, Y=Y, RB=RB, Dd=Dd, n=n, T=T, R=R, L=L, Q=Q, W=W, G=G, NG=NG, NC=NC, scaling=float((T * n) ** -0.5))
    rows = n * R
    vm = lambda shape, dtype=BF16: pltpu.VMEM(shape, dtype)
    dma = lambda *shape: pltpu.SemaphoreType.DMA(shape)
    any_spec = pl.BlockSpec(memory_space=pl.ANY)
    vm_spec = pl.BlockSpec(memory_space=pltpu.VMEM)
    outs = [
        ((T, Dd), BF16),
        ((T, Dd), BF16),
        (gate.shape, BF16),
        (up.shape, BF16),
        (down.shape, BF16),
        ((RB, Dd), F32),
        ((RB, Dd), F32),
    ]
    scratch = [
        vm((U, T, Dd)),
        vm((Dd, L)),
        vm((L, Dd)),
        vm((L, Hs)),
        vm((L, Hs)),
        vm((Hs, L)),
        vm((U, T, Dd)),
        vm((T, Dd)),
        vm((T, Dd)),
        vm((L, Hs)),
        vm((L, Hs)),
        vm((Hs, L)),
        vm((2, T, L)),
        vm((2, U, 2, RB, T)),
        vm((2, 4 * U, 2, RB, T)),
        vm((2, Z, RB, Dd)),
        vm((2, Z, RB, Dd)),
        vm((2, Z, RB, Dd), F32),
        vm((2, 4, T, Q)),
        vm((2, 4, T, Q)),
        vm((n, T), jnp.int32),
        vm((n, T), F32),
        vm((2 * rows, 2 * T)),
        vm((2 * rows, 2 * T)),
        vm((2 * rows, 2 * T)),
        vm((2, 8 * R, 8 * R)),
        vm((2, n, 2 * R, W)),
        vm((2, n, 2 * R, W)),
        vm((2, n, 2 * R, W)),
        vm((2, n, 2 * R, W)),
        vm((2, 4, rows, Q)),
        vm((2, 4, rows, Q)),
        vm((2, 2, rows, W)),
        vm((2, 2, rows, Q)),
        vm((rows, Hs), F32),
        vm((rows, Hs), F32),
        vm((rows, Hs)),
        vm((rows, Hs)),
        vm((rows, Hs)),
        dma(7),
        dma(7),
        dma(2, 4),
        dma(2, 4),
        dma(4),
        dma(4, NG),
        dma(2, NG, 4),
        dma(2, NG, 4),
        dma(2, NC, 6),
        dma(2, NC, 6),
        dma(2, 4),
        dma(2, 4),
        dma(2, Y),
        dma(2, Y),
        dma(2, Y),
        dma(2, Y),
        dma(2),
        dma(2),
        dma(2, 2, Z),
        dma(2, 2, Z),
        pltpu.SemaphoreType.REGULAR,
        pltpu.SemaphoreType.REGULAR,
    ]
    flops = 2 * rows * L * Hs * 9 + 2 * T * L * Dd * 4
    return pl.pallas_call(
        functools.partial(layer_kernel, cfg),
        out_shape=[jax.ShapeDtypeStruct(s, d) for s, d in outs],
        in_specs=[vm_spec] * 3 + [any_spec] * 7,
        out_specs=[any_spec] * len(outs),
        scratch_shapes=scratch,
        compiler_params=pltpu.CompilerParams(
            collective_id=0, has_side_effects=True, vmem_limit_bytes=62 * 1024 * 1024
        ),
        cost_estimate=pl.CostEstimate(flops=flops, bytes_accessed=16 * 2**20, transcendentals=rows * Hs),
    )(routes.T, slot_index.T, route_gates.T, tokens, to_latent, from_latent, gate, up, down, grad_output)


def local(
    tokens,
    to_latent,
    from_latent,
    expert_gate,
    expert_up,
    expert_down,
    routes,
    slot_index,
    route_gates,
    grad_output,
):
    expert_count = lax.axis_size("expert")
    dp_count = lax.axis_size("dp")
    token_count, route_count = routes.shape
    capacity = dp_count * max(
        1,
        min(
            token_count // (4 * dp_count),
            5 * token_count * route_count // (4 * expert_count * dp_count),
        ),
    )
    results = layer_call(
        capacity,
        expert_count,
        routes,
        slot_index,
        route_gates,
        tokens,
        to_latent,
        from_latent,
        expert_gate,
        expert_up,
        expert_down,
        grad_output,
    )
    layer_output, grad_tokens, grad_gate, grad_up, grad_down, grad_to_latent, grad_from_latent = copied(results)
    return (
        layer_output,
        grad_tokens,
        grad_to_latent,
        grad_from_latent,
        grad_gate,
        grad_up,
        grad_down,
    )


def solution(mesh):
    return jax.shard_map(
        local,
        mesh=mesh,
        in_specs=(
            P("expert", "dp"),
            P("dp", None),
            P(None, "dp"),
            P("expert", None, "dp"),
            P("expert", None, "dp"),
            P("expert", "dp", None),
            P("expert", None),
            P("expert", None),
            P("expert", None),
            P("expert", "dp"),
        ),
        out_specs=(
            P("expert", "dp"),
            P("expert", "dp"),
            P("expert", "dp"),
            P("expert", "dp"),
            P("expert", None, "dp"),
            P("expert", None, "dp"),
            P("expert", "dp", None),
        ),
        check_vma=False,
    )
```

```python
import functools

import jax
import jax.numpy as jnp
from jax import lax
from jax.experimental import pallas as pl
from jax.experimental.pallas import tpu as pltpu
from jax.sharding import PartitionSpec as P

F32 = jnp.float32
BF16 = jnp.bfloat16
LAST = (((1,), (1,)), ((), ()))
FIRST = (((0,), (0,)), ((), ()))
MESH = pl.DeviceIdType.MESH


def remote(src, dst, send_sem, recv_sem, where):
    return pltpu.make_async_remote_copy(
        src_ref=src, dst_ref=dst, send_sem=send_sem, recv_sem=recv_sem, device_id=where, device_id_type=MESH
    )


def layer_kernel(
    cfg,
    routes_ref,
    slots_ref,
    gates_ref,
    tok_in,
    tl_in,
    fl_in,
    gate_in,
    up_in,
    down_in,
    go_in,
    lo_out,
    gt_out,
    gg_out,
    gu_out,
    gd_out,
    gtl_out,
    gfl_out,
    tok_g,
    tl_v,
    fl_v,
    gate_v,
    up_v,
    down_v,
    go_g,
    lo_v,
    gt_v,
    gg_v,
    gu_v,
    gd_v,
    lat_v,
    turned,
    taken,
    zsend,
    zrecv,
    gsum,
    xs_send_v,
    xs_recv_v,
    s_tab,
    g_tab,
    pp,
    pph,
    ppl,
    perm,
    outgoing,
    arrived,
    leaving,
    returned,
    full,
    part,
    relay,
    frm,
    pg_v,
    pu_v,
    hid_v,
    gpg_v,
    gpu_v,
    load_sem,
    store_sem,
    xs_ssem,
    xs_rsem,
    a2a_ssem,
    a2a_rsem,
    ag_ssem,
    ag_rsem,
    rs_ssem,
    rs_rsem,
    fin_ssem,
    fin_rsem,
    sib_ssem,
    sib_rsem,
    near_ssem,
    near_rsem,
    turn_ssem,
    turn_rsem,
    z_ssem,
    z_rsem,
    y_ready,
    core_ready,
):
    Z, Y, RB, Dd = cfg["Z"], cfg["Y"], cfg["RB"], cfg["Dd"]
    U = 2 * Y
    n, T, R, L, Q, W, G, NG, NC = (cfg[k] for k in ("n", "T", "R", "L", "Q", "W", "G", "NG", "NC"))
    scaling = cfg["scaling"]
    R2 = 2 * R
    RG = G * R
    RC = n * R // NC
    GC = NG // NC
    me = lax.axis_index("expert")
    x = lax.axis_index("dp")
    right = lax.rem(x + 1, 4)
    left = lax.rem(x + 3, 4)
    opp = lax.rem(x + 2, 4)
    peers = (right, left, opp)
    core = lax.rem(me, 2)
    y = lax.rem(lax.div(me, 2), Y)
    z = lax.div(me, 2 * Y)
    unit = y * 2 + core

    def at(zz, yy, cc):
        return (zz * Y + yy) * 2 + cc

    sibling = {"expert": at(z, y, 1 - core)}

    unit_bits = U.bit_length() - 1

    def offsets(i):
        v = i - U
        p = lax.shift_right_arithmetic(v, unit_bits + 1) + 1
        w = v & (2 * U - 1)
        paired = lax.shift_right_logical(w, 1)
        dz = jnp.where(v < 0, 0, jnp.where((p < Z // 2) & ((w & 1) == 1), Z - p, p))
        u = jnp.where(v < 0, i, jnp.where(p < Z // 2, paired, w))
        return dz, lax.shift_right_logical(u, 1), u & 1

    def target_of(i):
        dz, dy, dc = offsets(i)
        return at((z + dz) & (Z - 1), (y + dy) & (Y - 1), (core + dc) & 1)

    def source_of(i):
        dz, dy, dc = offsets(i)
        return at((z + 2 * Z - dz) & (Z - 1), (y + Y - dy) & (Y - 1), (core + dc) & 1)

    loads = [
        pltpu.make_async_copy(src, dst, load_sem.at[i])
        for i, (src, dst) in enumerate(
            (
                (tok_in, tok_g.at[0]),
                (tl_in, tl_v),
                (go_in, go_g.at[0]),
                (fl_in, fl_v),
                (gate_in.at[0], gate_v),
                (up_in.at[0], up_v),
                (down_in.at[0], down_v),
            )
        )
    ]
    for load in loads[:2]:
        load.start()

    def signal(sem, where):
        pl.semaphore_signal(sem, inc=1, device_id=where, device_id_type=MESH)

    barrier = pltpu.get_barrier_semaphore()
    for peer in peers:
        signal(barrier, {"dp": peer})
    signal(barrier, sibling)
    for step in range(1, Y):
        signal(barrier, {"expert": at(z, (y + step) & (Y - 1), core)})
    for step in range(1, Z):
        signal(barrier, {"expert": at((z + step) & (Z - 1), y, core)})
    near_count = 3 + 1 + (Y - 1) + (Z - 1)

    whose = target_of(lax.broadcasted_iota(jnp.int32, (n, T), 0))
    s_val = jnp.full((n, T), -1000, jnp.int32)
    g_val = jnp.zeros((n, T), F32)
    for j in range(routes_ref.shape[0]):
        slot = slots_ref[j : j + 1, :]
        match = (whose == routes_ref[j : j + 1, :]) & (slot < R)
        s_val = jnp.where(match, slot, s_val)
        g_val = jnp.where(match, gates_ref[j : j + 1, :], g_val)
    s_tab[...] = s_val
    g_tab[...] = g_val

    size = 4 * R2
    row = lax.broadcasted_iota(jnp.int32, (size, size), 0)
    col = lax.broadcasted_iota(jnp.int32, (size, size), 1)
    kk = jnp.where(row >= 2 * R2, jnp.where(row >= 3 * R2, 3, 2), jnp.where(row >= R2, 1, 0))
    rest = row - kk * R2
    half = jnp.where(rest >= R, 1, 0)
    perm[0] = jnp.where(col == half * (4 * R) + kk * R + rest - half * R, 1.0, 0.0).astype(BF16)
    kk = jnp.where(col >= 2 * R2, jnp.where(col >= 3 * R2, 3, 2), jnp.where(col >= R2, 1, 0))
    rest = col - kk * R2
    half = jnp.where(rest >= R, 1, 0)
    perm[1] = jnp.where(row == half * (4 * R) + kk * R + rest - half * R, 1.0, 0.0).astype(BF16)

    def xs_copy(ph, j):
        return remote(
            xs_send_v.at[ph, j], xs_recv_v.at[ph, x], xs_ssem.at[ph, j], xs_rsem.at[ph, x], {"dp": j}
        )

    def xs_start(ph, value):
        for j in range(4):
            xs_send_v[ph, j] = value[:, j * Q : (j + 1) * Q].astype(BF16)
        for peer in peers:
            xs_copy(ph, peer).start()

    def xs_finish(ph):
        total = xs_send_v[ph, x].astype(F32)
        for peer in peers:
            remote(
                xs_send_v.at[ph, x], xs_recv_v.at[ph, peer], xs_ssem.at[ph, peer], xs_rsem.at[ph, peer], {"dp": peer}
            ).wait_recv()
            total = total + xs_recv_v[ph, peer].astype(F32)
        total = total.astype(BF16)
        return jnp.concatenate([total[:, :W], total[:, W:]], axis=0)

    loads[0].wait()
    loads[1].wait()
    loads[2].start()
    loads[3].start()
    latent_part = jnp.dot(tok_g[0], tl_v[...], preferred_element_type=F32)
    pl.semaphore_wait(barrier, near_count)
    xs_start(0, latent_part)
    for step in range(1, Y):
        signal(y_ready, {"expert": at(z, (y + step) & (Y - 1), core)})
    loads[2].wait()
    loads[3].wait()
    for load in loads[4:]:
        load.start()
    xs_start(1, lax.dot_general(go_g[0], fl_v[...], LAST, preferred_element_type=F32))
    if Y > 1:
        pl.semaphore_wait(y_ready, Y - 1)
    signal(core_ready, sibling)

    r_iota = lax.broadcasted_iota(jnp.int32, (G, R2, T), 1)

    def spread_table(table, ks):
        return jnp.broadcast_to(table[ks, :].reshape(G, 1, T), (G, R2, T))

    def dispatch(ph, stacked):
        @pl.loop(0, NG)
        def _(g):
            ks = pl.ds(pl.multiple_of(g * G, G), G)
            rows = pl.ds(pl.multiple_of(g * G * R2, G * R2), G * R2)
            s8 = spread_table(s_tab, ks)
            matches = [s8 == r_iota - h * R for h in range(2)]

            def one_hot(value):
                return jnp.concatenate(
                    [jnp.where(match, value, 0.0).reshape(G * R2, T).astype(BF16) for match in matches], axis=1
                )

            if ph == 0:
                weight = one_hot(1.0)
                pp[rows, :] = weight
                block = jnp.dot(weight, stacked, preferred_element_type=F32)
            else:
                g8 = spread_table(g_tab, ks)
                g_hi = g8.astype(BF16).astype(F32)
                high, low = one_hot(g_hi), one_hot(g8 - g_hi)
                pph[rows, :] = high
                ppl[rows, :] = low
                block = jnp.dot(high, stacked, preferred_element_type=F32)
                block = block + jnp.dot(low, stacked, preferred_element_type=F32)
            outgoing[ph, ks] = block.reshape(G, R2, W).astype(BF16)

            @pl.loop(jnp.maximum(g * G, 1), g * G + G)
            def _(k):
                remote(
                    outgoing.at[ph, k],
                    arrived.at[ph, k],
                    a2a_ssem.at[ph],
                    a2a_rsem.at[ph, g],
                    {"expert": target_of(k)},
                ).start()

        arrived[ph, 0] = outgoing[ph, 0]

    latent_rows = xs_finish(0)
    pl.semaphore_wait(core_ready, 1)
    dispatch(0, latent_rows)

    def sib_copy(i, dy):
        ref = (tok_g, go_g)[i]
        dst = ref.at[(2 * dy + 1 - 2 * core + U) & (U - 1)]
        return remote(ref.at[2 * dy], dst, sib_ssem.at[i, dy], sib_rsem.at[i, dy], sibling)

    def sib_wait(i, dy):
        ref = (tok_g, go_g)[i]
        here = (2 * dy + 2 * core - 1 + U) & (U - 1)
        remote(ref.at[2 * dy], ref.at[here], sib_ssem.at[i, dy], sib_rsem.at[i, dy], sibling).wait_recv()

    def near_copy(i, dy):
        ref = (tok_g, go_g)[i]
        return remote(
            ref.at[0],
            ref.at[2 * dy],
            near_ssem.at[i, dy],
            near_rsem.at[i, dy],
            {"expert": at(z, (y + dy) & (Y - 1), core)},
        )

    def near_start(i):
        sib_copy(i, 0).start()
        for dy in range(1, Y):
            near_copy(i, dy).start()

    def near_forward(i):
        for dy in range(1, Y):
            near_copy(i, dy).wait_recv()
            sib_copy(i, dy).start()

    def near_finish(i):
        for dy in range(Y):
            sib_wait(i, dy)


    def a2a_wait(ph, buf, g):
        @pl.when(g == 0)
        def _():
            pltpu.make_async_copy(buf.at[1:G], buf.at[1:G], a2a_rsem.at[ph, 0]).wait()

        @pl.when(g != 0)
        def _():
            ks = pl.ds(pl.multiple_of(g * G, G), G)
            pltpu.make_async_copy(buf.at[ks], buf.at[ks], a2a_rsem.at[ph, g]).wait()

    def group_rows(g):
        return pl.ds(pl.multiple_of(g * RG, RG), RG)

    halves = (slice(0, W), slice(W, 2 * W))

    def ag_copy(ph, g, kind, q):
        src = full.at[ph, q, group_rows(g)]
        if kind >= 2:
            src = full.at[ph, q, group_rows(g), halves[kind - 2]]
        where = {"dp": right if kind % 2 == 0 else left}
        return remote(src, src, ag_ssem.at[ph, g, kind], ag_rsem.at[ph, g, kind], where)

    def ag_start(ph, g):
        a2a_wait(ph, arrived.at[ph], g)
        for sub in range(G // 4):
            ks = pl.ds(pl.multiple_of(g * G + sub * 4, 4), 4)
            block = arrived[ph, ks].astype(F32).reshape(4 * R2, W).astype(BF16)
            dense = jnp.dot(perm[1], block, preferred_element_type=F32).astype(BF16)
            rows = pl.ds(pl.multiple_of(g * RG + sub * 4 * R, 4 * R), 4 * R)
            full[ph, x, rows, 0:W] = dense[: 4 * R]
            full[ph, x, rows, W : 2 * W] = dense[4 * R :]
        ag_copy(ph, g, 0, x).start()
        ag_copy(ph, g, 1, x).start()

    def ag_forward(ph, g):
        ag_copy(ph, g, 0, left).wait_recv()
        ag_copy(ph, g, 2, left).start()
        ag_copy(ph, g, 1, right).wait_recv()
        ag_copy(ph, g, 3, right).start()

    def ag_finish(ph, g):
        ag_copy(ph, g, 2, opp).wait_recv()
        ag_copy(ph, g, 3, opp).wait_recv()

    def chunk_rows(c):
        return pl.ds(pl.multiple_of(c * RC, RC), RC)

    def rs_copy(ph, c, kind):
        rows = chunk_rows(c)
        src, dst, where = (
            (part.at[ph, opp, rows, halves[0]], relay.at[ph, 0, rows], left),
            (part.at[ph, opp, rows, halves[1]], relay.at[ph, 1, rows], right),
            (part.at[ph, left, rows, halves[1]], frm.at[ph, 1, rows, halves[1]], left),
            (part.at[ph, right, rows, halves[0]], frm.at[ph, 0, rows, halves[0]], right),
            (part.at[ph, left, rows, halves[0]], frm.at[ph, 1, rows, halves[0]], left),
            (part.at[ph, right, rows, halves[1]], frm.at[ph, 0, rows, halves[1]], right),
        )[kind]
        return remote(src, dst, rs_ssem.at[ph, c, kind], rs_rsem.at[ph, c, kind], {"dp": where})

    def rs_start(ph, c, value):
        for j in range(4):
            part[ph, j, chunk_rows(c)] = value[:, j * Q : (j + 1) * Q].astype(BF16)
        for kind in range(4):
            rs_copy(ph, c, kind).start()

    def rs_relay(ph, c):
        rows = chunk_rows(c)
        for kind, target in ((0, left), (1, right)):
            rs_copy(ph, c, kind).wait_recv()
            own = part[ph, target, rows, halves[kind]].astype(F32)
            part[ph, target, rows, halves[kind]] = (own + relay[ph, kind, rows].astype(F32)).astype(BF16)
            rs_copy(ph, c, 4 + kind).start()

    def rs_finish(ph, c):
        for kind in (2, 3, 4, 5):
            rs_copy(ph, c, kind).wait_recv()

        @pl.loop(0, GC * G // 4)
        def _(sub):
            base = c * (GC * G) + sub * 4
            rows = pl.ds(pl.multiple_of(base * R, 4 * R), 4 * R)
            total = part[ph, x, rows].astype(F32) + frm[ph, 0, rows].astype(F32) + frm[ph, 1, rows].astype(F32)
            total = total.astype(BF16)
            stacked = jnp.concatenate([total[:, :W], total[:, W:]], axis=0)
            block = jnp.dot(perm[0], stacked, preferred_element_type=F32)
            leaving[ph, pl.ds(pl.multiple_of(base, 4), 4)] = block.reshape(4, R2, W).astype(BF16)

            @pl.loop(jnp.maximum(base, 1), base + 4)
            def _(k):
                remote(
                    leaving.at[ph, k],
                    returned.at[ph, k],
                    a2a_ssem.at[2 + ph],
                    a2a_rsem.at[2 + ph, lax.div(k, G)],
                    {"expert": source_of(k)},
                ).start()

    def fwd(c):
        rows = chunk_rows(c)
        block = jnp.concatenate([full[0, j, rows] for j in range(4)], axis=1)
        pre_gate = jnp.dot(block, gate_v[...], preferred_element_type=F32)
        pre_up = jnp.dot(block, up_v[...], preferred_element_type=F32)
        pg_v[rows, :] = pre_gate
        pu_v[rows, :] = pre_up
        hidden = (pre_gate * jax.nn.sigmoid(pre_gate) * pre_up).astype(BF16)
        hid_v[rows, :] = hidden
        return jnp.dot(hidden, down_v[...], preferred_element_type=F32)

    def bwd(c):
        rows = chunk_rows(c)
        block = jnp.concatenate([full[1, j, rows] for j in range(4)], axis=1)
        grad_hidden = lax.dot_general(block, down_v[...], LAST, preferred_element_type=F32)
        pre_gate = pg_v[rows, :]
        pre_up = pu_v[rows, :]
        s = jax.nn.sigmoid(pre_gate)
        grad_gate = (grad_hidden * pre_up * (s * (1.0 + pre_gate * (1.0 - s)))).astype(BF16)
        grad_up = (grad_hidden * (pre_gate * s)).astype(BF16)
        gpg_v[rows, :] = grad_gate
        gpu_v[rows, :] = grad_up
        value = lax.dot_general(grad_gate, gate_v[...], LAST, preferred_element_type=F32)
        return value + lax.dot_general(grad_up, up_v[...], LAST, preferred_element_type=F32)

    grad_rows = xs_finish(1)
    ag_start(0, 0)
    dispatch(1, grad_rows)

    near_start(1)
    near_start(0)

    @pl.loop(1, NG)
    def _(g):
        ag_start(0, g)

        @pl.when(g > 1)
        def _():
            ag_forward(0, g - 2)

    for load in loads[4:]:
        load.wait()

    @pl.loop(0, NC)
    def _(c):
        for i in range(GC):
            g = c * GC + i
            ag_start(1, g)

            @pl.when(g > 1)
            def _():
                ag_forward(1, g - 2)

            @pl.when(g <= 1)
            def _():
                ag_forward(0, NG - 2 + g)

        for i in range(GC):
            ag_finish(0, c * GC + i)
        rs_start(0, c, fwd(c))

        @pl.when(c > 0)
        def _():
            rs_relay(0, c - 1)

    ag_forward(1, NG - 2)
    ag_forward(1, NG - 1)
    rs_relay(0, NC - 1)

    @pl.loop(0, NC)
    def _(step):
        c = NC - 1 - step
        for i in range(GC):
            ag_finish(1, c * GC + i)
        rs_start(1, c, bwd(c))
        rs_finish(0, step)

    returned[0, 0] = leaving[0, 0]
    near_forward(0)
    near_forward(1)

    def combine(ph, weights, order):
        def step(i, total):
            g = order(i)
            a2a_wait(2 + ph, returned.at[ph], g)
            ks = pl.ds(pl.multiple_of(g * G, G), G)
            rows = pl.ds(pl.multiple_of(g * G * R2, G * R2), G * R2)
            block = returned[ph, ks].astype(F32).reshape(G * R2, W).astype(BF16)
            for weight in weights:
                total = total + lax.dot_general(block, weight[rows, :], FIRST, preferred_element_type=F32)
            return total

        total = lax.fori_loop(0, NG, step, jnp.zeros((W, 2 * T), F32))
        for h in range(2):
            turned[ph, :, h] = total[:, h * T : (h + 1) * T].reshape(U, RB, T).astype(BF16)
        taken[ph, 0] = turned[ph, unit]

        @pl.loop(1, 4 * U)
        def _(m):
            turn_copy(ph, m).start()

        lat_v[ph, :, lanes_of(x)] = jnp.concatenate([total[:, :T].T, total[:, T:].T], axis=1).astype(BF16)
        for peer in peers:
            fin_copy(ph, x, peer, x).start()

    def turn_copy(ph, m):
        dx = m & 3
        there = (unit + lax.shift_right_logical(m, 2)) & (U - 1)
        where = {"dp": (x + dx) & 3, "expert": z * U + there}
        return remote(turned.at[ph, there], taken.at[ph, m], turn_ssem.at[ph], turn_rsem.at[ph], where)

    def turn_wait(ph, sem, buf):
        pltpu.make_async_copy(buf.at[ph, 1 : 4 * U], buf.at[ph, 1 : 4 * U], sem.at[ph]).wait()

    def lanes_of(q):
        return pl.ds(pl.multiple_of(q * Q, Q), Q)

    def fin_copy(ph, q, peer, slot):
        src = lat_v.at[ph, :, lanes_of(q)]
        return remote(src, src, fin_ssem.at[ph, peer], fin_rsem.at[ph, slot], {"dp": peer})

    def fin_finish(ph):
        for peer in peers:
            fin_copy(ph, peer, peer, peer).wait_recv()

    cols = Dd // 2

    def col_chunk(c):
        return slice(c * cols, (c + 1) * cols)

    def z_copy(ph, c, step, source, target):
        return remote(
            zsend.at[ph, target, :, col_chunk(c)],
            zrecv.at[ph, source, :, col_chunk(c)],
            z_ssem.at[ph, c, step],
            z_rsem.at[ph, c, step],
            {"expert": at(target, y, core)},
        )

    def z_start(ph):
        near_finish(1 - ph)
        turn_wait(ph, turn_rsem, taken)
        other = (go_g, tok_g)[ph]
        left_side = jnp.concatenate(
            [taken[ph, 4 * u : 4 * u + 4].reshape(Z * RB, T) for u in range(U)], axis=1
        )
        for c in range(2):
            here = col_chunk(c)
            right_side = other[:, :, here].reshape(U * T, cols)
            value = jnp.dot(left_side, right_side, preferred_element_type=F32).reshape(4, 2, RB, cols)
            for dx in range(4):
                first = 2 * ((x + 4 - dx) & 3)
                gsum[ph, pl.ds(first, 2), :, here] = value[dx]
                zsend[ph, pl.ds(first, 2), :, here] = value[dx].astype(BF16)
            for step in range(1, Z):
                z_copy(ph, c, step, z, (z + step) & (Z - 1)).start()

    def z_finish(ph):
        for c in range(2):
            here = col_chunk(c)
            total = gsum[ph, z, :, here]
            for step in range(1, Z):
                source = (z + Z - step) & (Z - 1)
                z_copy(ph, c, step, source, z).wait_recv()
                total = total + zrecv[ph, source, :, here].astype(F32)
            gsum[ph, z, :, here] = total * scaling
        store(gsum.at[ph, z], (gfl_out, gtl_out)[ph])

    stores = []

    def store(src, dst):
        copy = pltpu.make_async_copy(src, dst, store_sem.at[len(stores)])
        copy.start()
        stores.append(copy)

    def grad_in(first, last):
        @pl.loop(first, last)
        def _(j):
            rows = pl.ds(pl.multiple_of(j * Q, Q), Q)
            block = full[0, j]
            for weight, result in ((gpg_v, gg_v), (gpu_v, gu_v)):
                value = lax.dot_general(block, weight[...], FIRST, preferred_element_type=F32)
                result[rows, :] = (value * scaling).astype(BF16)

    def grad_back(first, last):
        @pl.loop(first, last)
        def _(j):
            rows = pl.ds(pl.multiple_of(j * Q, Q), Q)
            value = lax.dot_general(hid_v[...], full[1, j], FIRST, preferred_element_type=F32)
            gd_v[:, rows] = (value * scaling).astype(BF16)

    rs_relay(1, NC - 1)
    grad_in(0, 2)
    for c in range(NC - 2, -1, -1):
        rs_relay(1, c)
        if c == NC - 2:
            grad_in(2, 4)
        if c > 0:
            rs_finish(1, c + 1)
    combine(0, (pph, ppl), lambda i: i)
    rs_finish(1, 1)
    rs_finish(1, 0)
    returned[1, 0] = leaving[1, 0]
    store(gg_v, gg_out.at[0])
    store(gu_v, gu_out.at[0])
    fin_finish(0)
    lo_v[...] = jnp.dot(lat_v[0], fl_v[...], preferred_element_type=F32).astype(BF16)
    store(lo_v, lo_out)
    z_start(0)
    combine(1, (pp,), lambda i: NG - 1 - i)
    grad_back(0, 4)
    store(gd_v, gd_out.at[0])
    z_finish(0)
    z_start(1)
    fin_finish(1)
    gt_v[...] = lax.dot_general(lat_v[1], tl_v[...], LAST, preferred_element_type=F32).astype(BF16)
    store(gt_v, gt_out)
    z_finish(1)

    for ph in range(2):
        for peer in peers:
            xs_copy(ph, peer).wait_send()
        for dy in range(Y):
            sib_copy(ph, dy).wait_send()
        for dy in range(1, Y):
            near_copy(ph, dy).wait_send()
        for peer in peers:
            fin_copy(ph, x, peer, x).wait_send()
        turn_wait(ph, turn_ssem, taken)
        for c in range(2):
            for step in range(1, Z):
                z_copy(ph, c, step, z, (z + step) & (Z - 1)).wait_send()
        for buf, sem in ((outgoing.at[ph], a2a_ssem.at[ph]), (leaving.at[ph], a2a_ssem.at[2 + ph])):
            pltpu.make_async_copy(buf.at[1:n], buf.at[1:n], sem).wait()

        @pl.loop(0, NG)
        def _(g):
            for kind, q in ((0, x), (1, x), (2, left), (3, right)):
                ag_copy(ph, g, kind, q).wait_send()

        @pl.loop(0, NC)
        def _(c):
            for kind in range(6):
                rs_copy(ph, c, kind).wait_send()

    for copy in stores:
        copy.wait()


def copy_kernel(count, *refs):
    sources, targets, held = refs[:count], refs[count : 2 * count], refs[2 * count : 3 * count]
    into, out = refs[3 * count :]
    first = [pltpu.make_async_copy(sources[i], held[i], into.at[i]) for i in range(count)]
    second = [pltpu.make_async_copy(held[i], targets[i], out.at[i]) for i in range(count)]
    for copy in first:
        copy.start()
    for i in range(count):
        first[i].wait()
        second[i].start()
    for copy in second:
        copy.wait()


def copied(arrays):
    count = len(arrays)
    any_spec = pl.BlockSpec(memory_space=pl.ANY)
    return pl.pallas_call(
        functools.partial(copy_kernel, count),
        out_shape=[jax.ShapeDtypeStruct(a.shape, a.dtype) for a in arrays],
        in_specs=[any_spec] * count,
        out_specs=[any_spec] * count,
        scratch_shapes=[pltpu.VMEM(a.shape, a.dtype) for a in arrays] + [pltpu.SemaphoreType.DMA((count,))] * 2,
        compiler_params=pltpu.CompilerParams(vmem_limit_bytes=62 * 1024 * 1024),
        cost_estimate=pl.CostEstimate(flops=0, bytes_accessed=8 * 2**20, transcendentals=0),
    )(*arrays)


def layer_call(capacity, n, routes, slot_index, route_gates, tokens, to_latent, from_latent, gate, up, down, grad_output):
    T, Dd = tokens.shape
    L = to_latent.shape[1]
    Hs = gate.shape[2]
    Q, W = L // 4, L // 8
    R = capacity
    G = 8 if n >= 16 else 4
    NG = n // G
    NC = min(4, NG)
    Z, RB = 8, L // n
    Y = n // (2 * Z)
    U = 2 * Y
    cfg = dict(Z=Z, Y=Y, RB=RB, Dd=Dd, n=n, T=T, R=R, L=L, Q=Q, W=W, G=G, NG=NG, NC=NC, scaling=float((T * n) ** -0.5))
    rows = n * R
    vm = lambda shape, dtype=BF16: pltpu.VMEM(shape, dtype)
    dma = lambda *shape: pltpu.SemaphoreType.DMA(shape)
    any_spec = pl.BlockSpec(memory_space=pl.ANY)
    vm_spec = pl.BlockSpec(memory_space=pltpu.VMEM)
    outs = [
        ((T, Dd), BF16),
        ((T, Dd), BF16),
        (gate.shape, BF16),
        (up.shape, BF16),
        (down.shape, BF16),
        ((RB, Dd), F32),
        ((RB, Dd), F32),
    ]
    scratch = [
        vm((U, T, Dd)),
        vm((Dd, L)),
        vm((L, Dd)),
        vm((L, Hs)),
        vm((L, Hs)),
        vm((Hs, L)),
        vm((U, T, Dd)),
        vm((T, Dd)),
        vm((T, Dd)),
        vm((L, Hs)),
        vm((L, Hs)),
        vm((Hs, L)),
        vm((2, T, L)),
        vm((2, U, 2, RB, T)),
        vm((2, 4 * U, 2, RB, T)),
        vm((2, Z, RB, Dd)),
        vm((2, Z, RB, Dd)),
        vm((2, Z, RB, Dd), F32),
        vm((2, 4, T, Q)),
        vm((2, 4, T, Q)),
        vm((n, T), jnp.int32),
        vm((n, T), F32),
        vm((2 * rows, 2 * T)),
        vm((2 * rows, 2 * T)),
        vm((2 * rows, 2 * T)),
        vm((2, 8 * R, 8 * R)),
        vm((2, n, 2 * R, W)),
        vm((2, n, 2 * R, W)),
        vm((2, n, 2 * R, W)),
        vm((2, n, 2 * R, W)),
        vm((2, 4, rows, Q)),
        vm((2, 4, rows, Q)),
        vm((2, 2, rows, W)),
        vm((2, 2, rows, Q)),
        vm((rows, Hs), F32),
        vm((rows, Hs), F32),
        vm((rows, Hs)),
        vm((rows, Hs)),
        vm((rows, Hs)),
        dma(7),
        dma(7),
        dma(2, 4),
        dma(2, 4),
        dma(4),
        dma(4, NG),
        dma(2, NG, 4),
        dma(2, NG, 4),
        dma(2, NC, 6),
        dma(2, NC, 6),
        dma(2, 4),
        dma(2, 4),
        dma(2, Y),
        dma(2, Y),
        dma(2, Y),
        dma(2, Y),
        dma(2),
        dma(2),
        dma(2, 2, Z),
        dma(2, 2, Z),
        pltpu.SemaphoreType.REGULAR,
        pltpu.SemaphoreType.REGULAR,
    ]
    flops = 2 * rows * L * Hs * 9 + 2 * T * L * Dd * 4
    return pl.pallas_call(
        functools.partial(layer_kernel, cfg),
        out_shape=[jax.ShapeDtypeStruct(s, d) for s, d in outs],
        in_specs=[vm_spec] * 3 + [any_spec] * 7,
        out_specs=[any_spec] * len(outs),
        scratch_shapes=scratch,
        compiler_params=pltpu.CompilerParams(
            collective_id=0, has_side_effects=True, vmem_limit_bytes=62 * 1024 * 1024
        ),
        cost_estimate=pl.CostEstimate(flops=flops, bytes_accessed=16 * 2**20, transcendentals=rows * Hs),
    )(routes.T, slot_index.T, route_gates.T, tokens, to_latent, from_latent, gate, up, down, grad_output)


def local(
    tokens,
    to_latent,
    from_latent,
    expert_gate,
    expert_up,
    expert_down,
    routes,
    slot_index,
    route_gates,
    grad_output,
):
    expert_count = lax.axis_size("expert")
    dp_count = lax.axis_size("dp")
    token_count, route_count = routes.shape
    capacity = dp_count * max(
        1,
        min(
            token_count // (4 * dp_count),
            5 * token_count * route_count // (4 * expert_count * dp_count),
        ),
    )
    results = layer_call(
        capacity,
        expert_count,
        routes,
        slot_index,
        route_gates,
        tokens,
        to_latent,
        from_latent,
        expert_gate,
        expert_up,
        expert_down,
        grad_output,
    )
    layer_output, grad_tokens, grad_gate, grad_up, grad_down, grad_to_latent, grad_from_latent = copied(results)
    return (
        layer_output,
        grad_tokens,
        grad_to_latent,
        grad_from_latent,
        grad_gate,
        grad_up,
        grad_down,
    )


def solution(mesh):
    return jax.shard_map(
        local,
        mesh=mesh,
        in_specs=(
            P("expert", "dp"),
            P("dp", None),
            P(None, "dp"),
            P("expert", None, "dp"),
            P("expert", None, "dp"),
            P("expert", "dp", None),
            P("expert", None),
            P("expert", None),
            P("expert", None),
            P("expert", "dp"),
        ),
        out_specs=(
            P("expert", "dp"),
            P("expert", "dp"),
            P("expert", "dp"),
            P("expert", "dp"),
            P("expert", None, "dp"),
            P("expert", None, "dp"),
            P("expert", "dp", None),
        ),
        check_vma=False,
    )
```

```python
import functools

import jax
import jax.numpy as jnp
from jax import lax
from jax.experimental import pallas as pl
from jax.experimental.pallas import tpu as pltpu
from jax.sharding import PartitionSpec as P

F32 = jnp.float32
BF16 = jnp.bfloat16
LAST = (((1,), (1,)), ((), ()))
FIRST = (((0,), (0,)), ((), ()))
MESH = pl.DeviceIdType.MESH


def remote(src, dst, send_sem, recv_sem, where):
    return pltpu.make_async_remote_copy(
        src_ref=src, dst_ref=dst, send_sem=send_sem, recv_sem=recv_sem, device_id=where, device_id_type=MESH
    )


def layer_kernel(
    cfg,
    routes_ref,
    slots_ref,
    gates_ref,
    tok_in,
    tl_in,
    fl_in,
    gate_in,
    up_in,
    down_in,
    go_in,
    lo_out,
    gt_out,
    gg_out,
    gu_out,
    gd_out,
    gtl_out,
    gfl_out,
    tok_g,
    tl_v,
    fl_v,
    gate_v,
    up_v,
    down_v,
    go_g,
    lo_v,
    gt_v,
    gg_v,
    gu_v,
    gd_v,
    lat_v,
    turned,
    taken,
    zsend,
    zrecv,
    gsum,
    xs_send_v,
    xs_recv_v,
    s_tab,
    g_tab,
    pp,
    pph,
    ppl,
    perm,
    outgoing,
    arrived,
    leaving,
    returned,
    full,
    part,
    relay,
    frm,
    pg_v,
    pu_v,
    hid_v,
    gpg_v,
    gpu_v,
    load_sem,
    store_sem,
    xs_ssem,
    xs_rsem,
    a2a_ssem,
    a2a_rsem,
    ag_ssem,
    ag_rsem,
    rs_ssem,
    rs_rsem,
    fin_ssem,
    fin_rsem,
    sib_ssem,
    sib_rsem,
    near_ssem,
    near_rsem,
    turn_ssem,
    turn_rsem,
    z_ssem,
    z_rsem,
    y_ready,
    core_ready,
):
    Z, Y, RB, Dd = cfg["Z"], cfg["Y"], cfg["RB"], cfg["Dd"]
    U = 2 * Y
    n, T, R, L, Q, W, G, NG, NC = (cfg[k] for k in ("n", "T", "R", "L", "Q", "W", "G", "NG", "NC"))
    scaling = cfg["scaling"]
    R2 = 2 * R
    RG = G * R
    RC = n * R // NC
    GC = NG // NC
    me = lax.axis_index("expert")
    x = lax.axis_index("dp")
    right = lax.rem(x + 1, 4)
    left = lax.rem(x + 3, 4)
    opp = lax.rem(x + 2, 4)
    peers = (right, left, opp)
    core = lax.rem(me, 2)
    y = lax.rem(lax.div(me, 2), Y)
    z = lax.div(me, 2 * Y)
    unit = y * 2 + core

    def at(zz, yy, cc):
        return (zz * Y + yy) * 2 + cc

    sibling = {"expert": at(z, y, 1 - core)}

    unit_bits = U.bit_length() - 1

    def offsets(i):
        v = i - U
        p = lax.shift_right_arithmetic(v, unit_bits + 1) + 1
        w = v & (2 * U - 1)
        paired = lax.shift_right_logical(w, 1)
        dz = jnp.where(v < 0, 0, jnp.where((p < Z // 2) & ((w & 1) == 1), Z - p, p))
        u = jnp.where(v < 0, i, jnp.where(p < Z // 2, paired, w))
        return dz, lax.shift_right_logical(u, 1), u & 1

    def target_of(i):
        dz, dy, dc = offsets(i)
        return at((z + dz) & (Z - 1), (y + dy) & (Y - 1), (core + dc) & 1)

    def source_of(i):
        dz, dy, dc = offsets(i)
        return at((z + 2 * Z - dz) & (Z - 1), (y + Y - dy) & (Y - 1), (core + dc) & 1)

    loads = [
        pltpu.make_async_copy(src, dst, load_sem.at[i])
        for i, (src, dst) in enumerate(
            (
                (tok_in, tok_g.at[0]),
                (tl_in, tl_v),
                (go_in, go_g.at[0]),
                (fl_in, fl_v),
                (gate_in.at[0], gate_v),
                (up_in.at[0], up_v),
                (down_in.at[0], down_v),
            )
        )
    ]
    for load in loads[:2]:
        load.start()

    def signal(sem, where):
        pl.semaphore_signal(sem, inc=1, device_id=where, device_id_type=MESH)

    barrier = pltpu.get_barrier_semaphore()
    for peer in peers:
        signal(barrier, {"dp": peer})
    signal(barrier, sibling)
    for step in range(1, Y):
        signal(barrier, {"expert": at(z, (y + step) & (Y - 1), core)})
    for step in range(1, Z):
        signal(barrier, {"expert": at((z + step) & (Z - 1), y, core)})
    near_count = 3 + 1 + (Y - 1) + (Z - 1)

    whose = target_of(lax.broadcasted_iota(jnp.int32, (n, T), 0))
    s_val = jnp.full((n, T), -1000, jnp.int32)
    g_val = jnp.zeros((n, T), F32)
    for j in range(routes_ref.shape[0]):
        slot = slots_ref[j : j + 1, :]
        match = (whose == routes_ref[j : j + 1, :]) & (slot < R)
        s_val = jnp.where(match, slot, s_val)
        g_val = jnp.where(match, gates_ref[j : j + 1, :], g_val)
    s_tab[...] = s_val
    g_tab[...] = g_val

    size = 4 * R2
    row = lax.broadcasted_iota(jnp.int32, (size, size), 0)
    col = lax.broadcasted_iota(jnp.int32, (size, size), 1)
    kk = jnp.where(row >= 2 * R2, jnp.where(row >= 3 * R2, 3, 2), jnp.where(row >= R2, 1, 0))
    rest = row - kk * R2
    half = jnp.where(rest >= R, 1, 0)
    perm[0] = jnp.where(col == half * (4 * R) + kk * R + rest - half * R, 1.0, 0.0).astype(BF16)
    kk = jnp.where(col >= 2 * R2, jnp.where(col >= 3 * R2, 3, 2), jnp.where(col >= R2, 1, 0))
    rest = col - kk * R2
    half = jnp.where(rest >= R, 1, 0)
    perm[1] = jnp.where(row == half * (4 * R) + kk * R + rest - half * R, 1.0, 0.0).astype(BF16)

    def xs_copy(ph, j):
        return remote(
            xs_send_v.at[ph, j], xs_recv_v.at[ph, x], xs_ssem.at[ph, j], xs_rsem.at[ph, x], {"dp": j}
        )

    def xs_start(ph, value):
        for j in range(4):
            xs_send_v[ph, j] = value[:, j * Q : (j + 1) * Q].astype(BF16)
        for peer in peers:
            xs_copy(ph, peer).start()

    def xs_finish(ph):
        total = xs_send_v[ph, x].astype(F32)
        for peer in peers:
            remote(
                xs_send_v.at[ph, x], xs_recv_v.at[ph, peer], xs_ssem.at[ph, peer], xs_rsem.at[ph, peer], {"dp": peer}
            ).wait_recv()
            total = total + xs_recv_v[ph, peer].astype(F32)
        total = total.astype(BF16)
        return jnp.concatenate([total[:, :W], total[:, W:]], axis=0)

    loads[0].wait()
    loads[1].wait()
    loads[2].start()
    loads[3].start()
    latent_part = jnp.dot(tok_g[0], tl_v[...], preferred_element_type=F32)
    pl.semaphore_wait(barrier, near_count)
    xs_start(0, latent_part)
    for step in range(1, Y):
        signal(y_ready, {"expert": at(z, (y + step) & (Y - 1), core)})
    loads[2].wait()
    loads[3].wait()
    for load in loads[4:]:
        load.start()
    if Y > 1:
        pl.semaphore_wait(y_ready, Y - 1)
    signal(core_ready, sibling)

    r_iota = lax.broadcasted_iota(jnp.int32, (G, R2, T), 1)

    def spread_table(table, ks):
        return jnp.broadcast_to(table[ks, :].reshape(G, 1, T), (G, R2, T))

    def dispatch(ph, stacked):
        @pl.loop(0, NG)
        def _(g):
            ks = pl.ds(pl.multiple_of(g * G, G), G)
            rows = pl.ds(pl.multiple_of(g * G * R2, G * R2), G * R2)
            s8 = spread_table(s_tab, ks)
            matches = [s8 == r_iota - h * R for h in range(2)]

            def one_hot(value):
                return jnp.concatenate(
                    [jnp.where(match, value, 0.0).reshape(G * R2, T).astype(BF16) for match in matches], axis=1
                )

            if ph == 0:
                weight = one_hot(1.0)
                pp[rows, :] = weight
                block = jnp.dot(weight, stacked, preferred_element_type=F32)
            else:
                g8 = spread_table(g_tab, ks)
                g_hi = g8.astype(BF16).astype(F32)
                high, low = one_hot(g_hi), one_hot(g8 - g_hi)
                pph[rows, :] = high
                ppl[rows, :] = low
                block = jnp.dot(high, stacked, preferred_element_type=F32)
                block = block + jnp.dot(low, stacked, preferred_element_type=F32)
            outgoing[ph, ks] = block.reshape(G, R2, W).astype(BF16)

            @pl.loop(jnp.maximum(g * G, 1), g * G + G)
            def _(k):
                remote(
                    outgoing.at[ph, k],
                    arrived.at[ph, k],
                    a2a_ssem.at[ph],
                    a2a_rsem.at[ph, g],
                    {"expert": target_of(k)},
                ).start()

        arrived[ph, 0] = outgoing[ph, 0]

    latent_rows = xs_finish(0)
    pl.semaphore_wait(core_ready, 1)
    dispatch(0, latent_rows)
    xs_start(1, lax.dot_general(go_g[0], fl_v[...], LAST, preferred_element_type=F32))

    def sib_copy(i, dy):
        ref = (tok_g, go_g)[i]
        dst = ref.at[(2 * dy + 1 - 2 * core + U) & (U - 1)]
        return remote(ref.at[2 * dy], dst, sib_ssem.at[i, dy], sib_rsem.at[i, dy], sibling)

    def sib_wait(i, dy):
        ref = (tok_g, go_g)[i]
        here = (2 * dy + 2 * core - 1 + U) & (U - 1)
        remote(ref.at[2 * dy], ref.at[here], sib_ssem.at[i, dy], sib_rsem.at[i, dy], sibling).wait_recv()

    def near_copy(i, dy):
        ref = (tok_g, go_g)[i]
        return remote(
            ref.at[0],
            ref.at[2 * dy],
            near_ssem.at[i, dy],
            near_rsem.at[i, dy],
            {"expert": at(z, (y + dy) & (Y - 1), core)},
        )

    def near_start(i):
        sib_copy(i, 0).start()
        for dy in range(1, Y):
            near_copy(i, dy).start()

    def near_forward(i):
        for dy in range(1, Y):
            near_copy(i, dy).wait_recv()
            sib_copy(i, dy).start()

    def near_finish(i):
        for dy in range(Y):
            sib_wait(i, dy)


    def a2a_wait(ph, buf, g):
        @pl.when(g == 0)
        def _():
            pltpu.make_async_copy(buf.at[1:G], buf.at[1:G], a2a_rsem.at[ph, 0]).wait()

        @pl.when(g != 0)
        def _():
            ks = pl.ds(pl.multiple_of(g * G, G), G)
            pltpu.make_async_copy(buf.at[ks], buf.at[ks], a2a_rsem.at[ph, g]).wait()

    def group_rows(g):
        return pl.ds(pl.multiple_of(g * RG, RG), RG)

    halves = (slice(0, W), slice(W, 2 * W))

    def ag_copy(ph, g, kind, q):
        src = full.at[ph, q, group_rows(g)]
        if kind >= 2:
            src = full.at[ph, q, group_rows(g), halves[kind - 2]]
        where = {"dp": right if kind % 2 == 0 else left}
        return remote(src, src, ag_ssem.at[ph, g, kind], ag_rsem.at[ph, g, kind], where)

    def ag_start(ph, g):
        a2a_wait(ph, arrived.at[ph], g)
        for sub in range(G // 4):
            ks = pl.ds(pl.multiple_of(g * G + sub * 4, 4), 4)
            block = arrived[ph, ks].astype(F32).reshape(4 * R2, W).astype(BF16)
            dense = jnp.dot(perm[1], block, preferred_element_type=F32).astype(BF16)
            rows = pl.ds(pl.multiple_of(g * RG + sub * 4 * R, 4 * R), 4 * R)
            full[ph, x, rows, 0:W] = dense[: 4 * R]
            full[ph, x, rows, W : 2 * W] = dense[4 * R :]
        ag_copy(ph, g, 0, x).start()
        ag_copy(ph, g, 1, x).start()

    def ag_forward(ph, g):
        ag_copy(ph, g, 0, left).wait_recv()
        ag_copy(ph, g, 2, left).start()
        ag_copy(ph, g, 1, right).wait_recv()
        ag_copy(ph, g, 3, right).start()

    def ag_finish(ph, g):
        ag_copy(ph, g, 2, opp).wait_recv()
        ag_copy(ph, g, 3, opp).wait_recv()

    def chunk_rows(c):
        return pl.ds(pl.multiple_of(c * RC, RC), RC)

    def rs_copy(ph, c, kind):
        rows = chunk_rows(c)
        src, dst, where = (
            (part.at[ph, opp, rows, halves[0]], relay.at[ph, 0, rows], left),
            (part.at[ph, opp, rows, halves[1]], relay.at[ph, 1, rows], right),
            (part.at[ph, left, rows, halves[1]], frm.at[ph, 1, rows, halves[1]], left),
            (part.at[ph, right, rows, halves[0]], frm.at[ph, 0, rows, halves[0]], right),
            (part.at[ph, left, rows, halves[0]], frm.at[ph, 1, rows, halves[0]], left),
            (part.at[ph, right, rows, halves[1]], frm.at[ph, 0, rows, halves[1]], right),
        )[kind]
        return remote(src, dst, rs_ssem.at[ph, c, kind], rs_rsem.at[ph, c, kind], {"dp": where})

    def rs_start(ph, c, value):
        for j in range(4):
            part[ph, j, chunk_rows(c)] = value[:, j * Q : (j + 1) * Q].astype(BF16)
        for kind in range(4):
            rs_copy(ph, c, kind).start()

    def rs_relay(ph, c):
        rows = chunk_rows(c)
        for kind, target in ((0, left), (1, right)):
            rs_copy(ph, c, kind).wait_recv()
            own = part[ph, target, rows, halves[kind]].astype(F32)
            part[ph, target, rows, halves[kind]] = (own + relay[ph, kind, rows].astype(F32)).astype(BF16)
            rs_copy(ph, c, 4 + kind).start()

    def rs_finish(ph, c):
        for kind in (2, 3, 4, 5):
            rs_copy(ph, c, kind).wait_recv()

        @pl.loop(0, GC * G // 4)
        def _(sub):
            base = c * (GC * G) + sub * 4
            rows = pl.ds(pl.multiple_of(base * R, 4 * R), 4 * R)
            total = part[ph, x, rows].astype(F32) + frm[ph, 0, rows].astype(F32) + frm[ph, 1, rows].astype(F32)
            total = total.astype(BF16)
            stacked = jnp.concatenate([total[:, :W], total[:, W:]], axis=0)
            block = jnp.dot(perm[0], stacked, preferred_element_type=F32)
            leaving[ph, pl.ds(pl.multiple_of(base, 4), 4)] = block.reshape(4, R2, W).astype(BF16)

            @pl.loop(jnp.maximum(base, 1), base + 4)
            def _(k):
                remote(
                    leaving.at[ph, k],
                    returned.at[ph, k],
                    a2a_ssem.at[2 + ph],
                    a2a_rsem.at[2 + ph, lax.div(k, G)],
                    {"expert": source_of(k)},
                ).start()

    def fwd(c):
        rows = chunk_rows(c)
        block = jnp.concatenate([full[0, j, rows] for j in range(4)], axis=1)
        pre_gate = jnp.dot(block, gate_v[...], preferred_element_type=F32)
        pre_up = jnp.dot(block, up_v[...], preferred_element_type=F32)
        pg_v[rows, :] = pre_gate
        pu_v[rows, :] = pre_up
        hidden = (pre_gate * jax.nn.sigmoid(pre_gate) * pre_up).astype(BF16)
        hid_v[rows, :] = hidden
        return jnp.dot(hidden, down_v[...], preferred_element_type=F32)

    def bwd(c):
        rows = chunk_rows(c)
        block = jnp.concatenate([full[1, j, rows] for j in range(4)], axis=1)
        grad_hidden = lax.dot_general(block, down_v[...], LAST, preferred_element_type=F32)
        pre_gate = pg_v[rows, :]
        pre_up = pu_v[rows, :]
        s = jax.nn.sigmoid(pre_gate)
        grad_gate = (grad_hidden * pre_up * (s * (1.0 + pre_gate * (1.0 - s)))).astype(BF16)
        grad_up = (grad_hidden * (pre_gate * s)).astype(BF16)
        gpg_v[rows, :] = grad_gate
        gpu_v[rows, :] = grad_up
        value = lax.dot_general(grad_gate, gate_v[...], LAST, preferred_element_type=F32)
        return value + lax.dot_general(grad_up, up_v[...], LAST, preferred_element_type=F32)

    grad_rows = xs_finish(1)
    ag_start(0, 0)
    dispatch(1, grad_rows)

    near_start(1)
    near_start(0)

    @pl.loop(1, NG)
    def _(g):
        ag_start(0, g)

        @pl.when(g > 1)
        def _():
            ag_forward(0, g - 2)

    for load in loads[4:]:
        load.wait()

    @pl.loop(0, NC)
    def _(c):
        for i in range(GC):
            g = c * GC + i
            ag_start(1, g)

            @pl.when(g > 1)
            def _():
                ag_forward(1, g - 2)

            @pl.when(g <= 1)
            def _():
                ag_forward(0, NG - 2 + g)

        for i in range(GC):
            ag_finish(0, c * GC + i)
        rs_start(0, c, fwd(c))

        @pl.when(c > 0)
        def _():
            rs_relay(0, c - 1)

    ag_forward(1, NG - 2)
    ag_forward(1, NG - 1)
    rs_relay(0, NC - 1)

    @pl.loop(0, NC)
    def _(step):
        c = NC - 1 - step
        for i in range(GC):
            ag_finish(1, c * GC + i)
        rs_start(1, c, bwd(c))
        rs_finish(0, step)

    returned[0, 0] = leaving[0, 0]
    near_forward(0)
    near_forward(1)

    def combine(ph, weights, order):
        def step(i, total):
            g = order(i)
            a2a_wait(2 + ph, returned.at[ph], g)
            ks = pl.ds(pl.multiple_of(g * G, G), G)
            rows = pl.ds(pl.multiple_of(g * G * R2, G * R2), G * R2)
            block = returned[ph, ks].astype(F32).reshape(G * R2, W).astype(BF16)
            for weight in weights:
                total = total + lax.dot_general(block, weight[rows, :], FIRST, preferred_element_type=F32)
            return total

        total = lax.fori_loop(0, NG, step, jnp.zeros((W, 2 * T), F32))
        for h in range(2):
            turned[ph, :, h] = total[:, h * T : (h + 1) * T].reshape(U, RB, T).astype(BF16)
        taken[ph, 0] = turned[ph, unit]

        @pl.loop(1, 4 * U)
        def _(m):
            turn_copy(ph, m).start()

        lat_v[ph, :, lanes_of(x)] = jnp.concatenate([total[:, :T].T, total[:, T:].T], axis=1).astype(BF16)
        for peer in peers:
            fin_copy(ph, x, peer, x).start()

    def turn_copy(ph, m):
        dx = m & 3
        there = (unit + lax.shift_right_logical(m, 2)) & (U - 1)
        where = {"dp": (x + dx) & 3, "expert": z * U + there}
        return remote(turned.at[ph, there], taken.at[ph, m], turn_ssem.at[ph], turn_rsem.at[ph], where)

    def turn_wait(ph, sem, buf):
        pltpu.make_async_copy(buf.at[ph, 1 : 4 * U], buf.at[ph, 1 : 4 * U], sem.at[ph]).wait()

    def lanes_of(q):
        return pl.ds(pl.multiple_of(q * Q, Q), Q)

    def fin_copy(ph, q, peer, slot):
        src = lat_v.at[ph, :, lanes_of(q)]
        return remote(src, src, fin_ssem.at[ph, peer], fin_rsem.at[ph, slot], {"dp": peer})

    def fin_finish(ph):
        for peer in peers:
            fin_copy(ph, peer, peer, peer).wait_recv()

    cols = Dd // 2

    def col_chunk(c):
        return slice(c * cols, (c + 1) * cols)

    def z_copy(ph, c, step, source, target):
        return remote(
            zsend.at[ph, target, :, col_chunk(c)],
            zrecv.at[ph, source, :, col_chunk(c)],
            z_ssem.at[ph, c, step],
            z_rsem.at[ph, c, step],
            {"expert": at(target, y, core)},
        )

    def z_start(ph):
        near_finish(1 - ph)
        turn_wait(ph, turn_rsem, taken)
        other = (go_g, tok_g)[ph]
        left_side = jnp.concatenate(
            [taken[ph, 4 * u : 4 * u + 4].reshape(Z * RB, T) for u in range(U)], axis=1
        )
        for c in range(2):
            here = col_chunk(c)
            right_side = other[:, :, here].reshape(U * T, cols)
            value = jnp.dot(left_side, right_side, preferred_element_type=F32).reshape(4, 2, RB, cols)
            for dx in range(4):
                first = 2 * ((x + 4 - dx) & 3)
                gsum[ph, pl.ds(first, 2), :, here] = value[dx]
                zsend[ph, pl.ds(first, 2), :, here] = value[dx].astype(BF16)
            for step in range(1, Z):
                z_copy(ph, c, step, z, (z + step) & (Z - 1)).start()

    def z_finish(ph):
        for c in range(2):
            here = col_chunk(c)
            total = gsum[ph, z, :, here]
            for step in range(1, Z):
                source = (z + Z - step) & (Z - 1)
                z_copy(ph, c, step, source, z).wait_recv()
                total = total + zrecv[ph, source, :, here].astype(F32)
            gsum[ph, z, :, here] = total * scaling
        store(gsum.at[ph, z], (gfl_out, gtl_out)[ph])

    stores = []

    def store(src, dst):
        copy = pltpu.make_async_copy(src, dst, store_sem.at[len(stores)])
        copy.start()
        stores.append(copy)

    def grad_in(first, last):
        @pl.loop(first, last)
        def _(j):
            rows = pl.ds(pl.multiple_of(j * Q, Q), Q)
            block = full[0, j]
            for weight, result in ((gpg_v, gg_v), (gpu_v, gu_v)):
                value = lax.dot_general(block, weight[...], FIRST, preferred_element_type=F32)
                result[rows, :] = (value * scaling).astype(BF16)

    def grad_back(first, last):
        @pl.loop(first, last)
        def _(j):
            rows = pl.ds(pl.multiple_of(j * Q, Q), Q)
            value = lax.dot_general(hid_v[...], full[1, j], FIRST, preferred_element_type=F32)
            gd_v[:, rows] = (value * scaling).astype(BF16)

    rs_relay(1, NC - 1)
    grad_in(0, 2)
    for c in range(NC - 2, -1, -1):
        rs_relay(1, c)
        if c == NC - 2:
            grad_in(2, 4)
        if c > 0:
            rs_finish(1, c + 1)
    combine(0, (pph, ppl), lambda i: i)
    rs_finish(1, 1)
    rs_finish(1, 0)
    returned[1, 0] = leaving[1, 0]
    store(gg_v, gg_out.at[0])
    store(gu_v, gu_out.at[0])
    fin_finish(0)
    lo_v[...] = jnp.dot(lat_v[0], fl_v[...], preferred_element_type=F32).astype(BF16)
    store(lo_v, lo_out)
    z_start(0)
    combine(1, (pp,), lambda i: NG - 1 - i)
    grad_back(0, 4)
    store(gd_v, gd_out.at[0])
    z_finish(0)
    z_start(1)
    fin_finish(1)
    gt_v[...] = lax.dot_general(lat_v[1], tl_v[...], LAST, preferred_element_type=F32).astype(BF16)
    store(gt_v, gt_out)
    z_finish(1)

    for ph in range(2):
        for peer in peers:
            xs_copy(ph, peer).wait_send()
        for dy in range(Y):
            sib_copy(ph, dy).wait_send()
        for dy in range(1, Y):
            near_copy(ph, dy).wait_send()
        for peer in peers:
            fin_copy(ph, x, peer, x).wait_send()
        turn_wait(ph, turn_ssem, taken)
        for c in range(2):
            for step in range(1, Z):
                z_copy(ph, c, step, z, (z + step) & (Z - 1)).wait_send()
        for buf, sem in ((outgoing.at[ph], a2a_ssem.at[ph]), (leaving.at[ph], a2a_ssem.at[2 + ph])):
            pltpu.make_async_copy(buf.at[1:n], buf.at[1:n], sem).wait()

        @pl.loop(0, NG)
        def _(g):
            for kind, q in ((0, x), (1, x), (2, left), (3, right)):
                ag_copy(ph, g, kind, q).wait_send()

        @pl.loop(0, NC)
        def _(c):
            for kind in range(6):
                rs_copy(ph, c, kind).wait_send()

    for copy in stores:
        copy.wait()


def copy_kernel(count, *refs):
    sources, targets, held = refs[:count], refs[count : 2 * count], refs[2 * count : 3 * count]
    into, out = refs[3 * count :]
    first = [pltpu.make_async_copy(sources[i], held[i], into.at[i]) for i in range(count)]
    second = [pltpu.make_async_copy(held[i], targets[i], out.at[i]) for i in range(count)]
    for copy in first:
        copy.start()
    for i in range(count):
        first[i].wait()
        second[i].start()
    for copy in second:
        copy.wait()


def copied(arrays):
    count = len(arrays)
    any_spec = pl.BlockSpec(memory_space=pl.ANY)
    return pl.pallas_call(
        functools.partial(copy_kernel, count),
        out_shape=[jax.ShapeDtypeStruct(a.shape, a.dtype) for a in arrays],
        in_specs=[any_spec] * count,
        out_specs=[any_spec] * count,
        scratch_shapes=[pltpu.VMEM(a.shape, a.dtype) for a in arrays] + [pltpu.SemaphoreType.DMA((count,))] * 2,
        compiler_params=pltpu.CompilerParams(vmem_limit_bytes=62 * 1024 * 1024),
        cost_estimate=pl.CostEstimate(flops=0, bytes_accessed=8 * 2**20, transcendentals=0),
    )(*arrays)


def layer_call(capacity, n, routes, slot_index, route_gates, tokens, to_latent, from_latent, gate, up, down, grad_output):
    T, Dd = tokens.shape
    L = to_latent.shape[1]
    Hs = gate.shape[2]
    Q, W = L // 4, L // 8
    R = capacity
    G = 8 if n >= 16 else 4
    NG = n // G
    NC = min(4, NG)
    Z, RB = 8, L // n
    Y = n // (2 * Z)
    U = 2 * Y
    cfg = dict(Z=Z, Y=Y, RB=RB, Dd=Dd, n=n, T=T, R=R, L=L, Q=Q, W=W, G=G, NG=NG, NC=NC, scaling=float((T * n) ** -0.5))
    rows = n * R
    vm = lambda shape, dtype=BF16: pltpu.VMEM(shape, dtype)
    dma = lambda *shape: pltpu.SemaphoreType.DMA(shape)
    any_spec = pl.BlockSpec(memory_space=pl.ANY)
    vm_spec = pl.BlockSpec(memory_space=pltpu.VMEM)
    outs = [
        ((T, Dd), BF16),
        ((T, Dd), BF16),
        (gate.shape, BF16),
        (up.shape, BF16),
        (down.shape, BF16),
        ((RB, Dd), F32),
        ((RB, Dd), F32),
    ]
    scratch = [
        vm((U, T, Dd)),
        vm((Dd, L)),
        vm((L, Dd)),
        vm((L, Hs)),
        vm((L, Hs)),
        vm((Hs, L)),
        vm((U, T, Dd)),
        vm((T, Dd)),
        vm((T, Dd)),
        vm((L, Hs)),
        vm((L, Hs)),
        vm((Hs, L)),
        vm((2, T, L)),
        vm((2, U, 2, RB, T)),
        vm((2, 4 * U, 2, RB, T)),
        vm((2, Z, RB, Dd)),
        vm((2, Z, RB, Dd)),
        vm((2, Z, RB, Dd), F32),
        vm((2, 4, T, Q)),
        vm((2, 4, T, Q)),
        vm((n, T), jnp.int32),
        vm((n, T), F32),
        vm((2 * rows, 2 * T)),
        vm((2 * rows, 2 * T)),
        vm((2 * rows, 2 * T)),
        vm((2, 8 * R, 8 * R)),
        vm((2, n, 2 * R, W)),
        vm((2, n, 2 * R, W)),
        vm((2, n, 2 * R, W)),
        vm((2, n, 2 * R, W)),
        vm((2, 4, rows, Q)),
        vm((2, 4, rows, Q)),
        vm((2, 2, rows, W)),
        vm((2, 2, rows, Q)),
        vm((rows, Hs), F32),
        vm((rows, Hs), F32),
        vm((rows, Hs)),
        vm((rows, Hs)),
        vm((rows, Hs)),
        dma(7),
        dma(7),
        dma(2, 4),
        dma(2, 4),
        dma(4),
        dma(4, NG),
        dma(2, NG, 4),
        dma(2, NG, 4),
        dma(2, NC, 6),
        dma(2, NC, 6),
        dma(2, 4),
        dma(2, 4),
        dma(2, Y),
        dma(2, Y),
        dma(2, Y),
        dma(2, Y),
        dma(2),
        dma(2),
        dma(2, 2, Z),
        dma(2, 2, Z),
        pltpu.SemaphoreType.REGULAR,
        pltpu.SemaphoreType.REGULAR,
    ]
    flops = 2 * rows * L * Hs * 9 + 2 * T * L * Dd * 4
    return pl.pallas_call(
        functools.partial(layer_kernel, cfg),
        out_shape=[jax.ShapeDtypeStruct(s, d) for s, d in outs],
        in_specs=[vm_spec] * 3 + [any_spec] * 7,
        out_specs=[any_spec] * len(outs),
        scratch_shapes=scratch,
        compiler_params=pltpu.CompilerParams(
            collective_id=0, has_side_effects=True, vmem_limit_bytes=62 * 1024 * 1024
        ),
        cost_estimate=pl.CostEstimate(flops=flops, bytes_accessed=16 * 2**20, transcendentals=rows * Hs),
    )(routes.T, slot_index.T, route_gates.T, tokens, to_latent, from_latent, gate, up, down, grad_output)


def local(
    tokens,
    to_latent,
    from_latent,
    expert_gate,
    expert_up,
    expert_down,
    routes,
    slot_index,
    route_gates,
    grad_output,
):
    expert_count = lax.axis_size("expert")
    dp_count = lax.axis_size("dp")
    token_count, route_count = routes.shape
    capacity = dp_count * max(
        1,
        min(
            token_count // (4 * dp_count),
            5 * token_count * route_count // (4 * expert_count * dp_count),
        ),
    )
    results = layer_call(
        capacity,
        expert_count,
        routes,
        slot_index,
        route_gates,
        tokens,
        to_latent,
        from_latent,
        expert_gate,
        expert_up,
        expert_down,
        grad_output,
    )
    layer_output, grad_tokens, grad_gate, grad_up, grad_down, grad_to_latent, grad_from_latent = copied(results)
    return (
        layer_output,
        grad_tokens,
        grad_to_latent,
        grad_from_latent,
        grad_gate,
        grad_up,
        grad_down,
    )


def solution(mesh):
    return jax.shard_map(
        local,
        mesh=mesh,
        in_specs=(
            P("expert", "dp"),
            P("dp", None),
            P(None, "dp"),
            P("expert", None, "dp"),
            P("expert", None, "dp"),
            P("expert", "dp", None),
            P("expert", None),
            P("expert", None),
            P("expert", None),
            P("expert", "dp"),
        ),
        out_specs=(
            P("expert", "dp"),
            P("expert", "dp"),
            P("expert", "dp"),
            P("expert", "dp"),
            P("expert", None, "dp"),
            P("expert", None, "dp"),
            P("expert", "dp", None),
        ),
        check_vma=False,
    )
```
